768 devices in a mesh: grp: 24 (over z, core), peer: 32 (over y, x).
Axes of the slice: x: 4, y: 8, z: 12, core: 2. Of those that a mesh axis runs over, the one named last changes fastest.
Arguments:
- descriptors: bfloat16 [196608, 256], P(('grp', 'peer'))
- cell_ids: int32 [196608], P(('grp', 'peer')), may hold values from 0 to 63, as said below
- sub_codes: int32 [196608, 32], P(('grp', 'peer')), may hold values from 0 to 255
- centroids: bfloat16 [1536, 256], P(('grp', 'peer')), may hold values from -3 to 3
- codebooks: bfloat16 [1536, 256, 256], P(('grp', 'peer')), may hold values from -6 to 6
Outputs:
- rotated: bfloat16 [196608, 256], P(('grp', 'peer'))
- rotations: float32 [1536, 256, 256], P(('grp', 'peer'))
- distortion: float32 [], replicated
The draws below stay inside these ranges and needn't reach their ends.
Inputs may be any that keep to these rules, and one draw needn't show every extreme that they name: `cell_ids`: rows of one group name only that group's cells; cell l of a group is owned by its peer l // 2. From one device at most 8 rows name one cell and at most 10 rows name cells of one owner. In every group one cell gets exactly 8 rows from every device of the group, and its owner exactly 10 rows from every device.
All inputs are finite; a program needn't handle non-finite values.
Results may differ from the reference program's by a relative error of at most 0.0046.
Values may be sent and summed in bfloat16 or wider, within the bound.
A program may use at most 32 MiB of HBM per device.

```python
import jax
import jax.numpy as jnp
from jax import lax

D = 256
SUB = 32
CODES = 256
CPO = 2
NEWTON = 3
ROWS_DEV = 256
MOST = 8
OWN = 10
ROWS = 196608
CELLS = 1536
N_GRP = 24
N_PEER = 32


def cell_layout(key):
    owner_key, cell_key, first_key, second_key, order_key = jax.random.split(key, 5)
    forced_owner = jax.random.randint(owner_key, (N_GRP,), 0, N_PEER)
    forced_cell = jax.random.randint(cell_key, (N_GRP,), 0, CPO)
    candidates = CPO * MOST
    entries = jnp.arange(candidates, dtype=jnp.int32)
    entry_cell = entries // MOST
    owners = jnp.arange(N_PEER, dtype=jnp.int32)
    noise_first = jax.random.randint(first_key, (N_GRP, N_PEER, N_PEER, candidates), 0, 65536)
    favoured = (owners[None, None, :, None] == forced_owner[:, None, None, None]) & (entry_cell[None, None, None, :] == forced_cell[:, None, None, None])
    score_first = favoured.astype(jnp.int32) * (1 << 28) + noise_first * candidates + entries
    chosen = jnp.argsort(-score_first, axis=-1)[..., :OWN]
    chosen_cell = entry_cell[chosen] + owners[None, None, :, None] * CPO
    flat_cells = chosen_cell.reshape(N_GRP, N_PEER, N_PEER * OWN)
    slot_ids = jnp.arange(N_PEER * OWN, dtype=jnp.int32)
    noise_second = jax.random.randint(second_key, (N_GRP, N_PEER, N_PEER * OWN), 0, 65536)
    favoured_owner = slot_ids[None, None, :] // OWN == forced_owner[:, None, None]
    score_second = favoured_owner.astype(jnp.int32) * (1 << 29) + noise_second * (N_PEER * OWN) + slot_ids
    picked = jnp.argsort(-score_second, axis=-1)[..., :ROWS_DEV]
    picked_cells = jnp.take_along_axis(flat_cells, picked, axis=-1)
    noise_order = jax.random.randint(order_key, (N_GRP, N_PEER, ROWS_DEV), 0, 65536) * ROWS_DEV + jnp.arange(ROWS_DEV, dtype=jnp.int32)
    shuffle = jnp.argsort(noise_order, axis=-1)
    return jnp.take_along_axis(picked_cells, shuffle, axis=-1).reshape(ROWS).astype(jnp.int32)


def draw_cell_ids(key, part):
    return cell_layout(key)


def draw_descriptors(key, part):
    labels = cell_layout(key)
    key = jax.random.fold_in(key, 7)
    row_group = jnp.arange(ROWS, dtype=jnp.int32) // (ROWS_DEV * N_PEER)
    owner_global = row_group * N_PEER + labels // CPO
    position = owner_global.astype(jnp.float32) / float(max(N_GRP * N_PEER - 1, 1))
    row_scale = 1.0 + 2.0 * position
    return (row_scale[:, None] * jax.random.normal(key, (ROWS, D), jnp.float32)).astype(jnp.bfloat16)


def with_ends(result, own_key, least, top_value):
    place = [jax.random.randint(jax.random.fold_in(own_key, axis), (), 0, length) for axis, length in enumerate(result.shape)]
    longest = result.shape.index(max(result.shape))
    next_to = place[:longest] + [(place[longest] + 1) % result.shape[longest]] + place[longest + 1:]
    return result.at[tuple(place)].set(least).at[tuple(next_to)].set(top_value)


def shard_levels(own_key, dims, shards, low, largest):
    level, own = 1.0, jax.random.fold_in(own_key, 6)
    for dim, parts in shards:
        steps = jnp.exp(jax.random.uniform(jax.random.fold_in(own, dim), (parts,), jnp.float32, low / len(shards), largest / len(shards)))
        level = level * jnp.repeat(steps, dims[dim] // parts).reshape([-1 if axis == dim else 1 for axis in range(len(dims))])
    return level


def gaussian(stream_key, extent, width, limit, cuts=(), kind=jnp.bfloat16):
    drawn = width * jax.random.normal(stream_key, extent, jnp.float32)
    if cuts:
        drawn = drawn * shard_levels(stream_key, extent, cuts, -0.22, 0.18)
    return jnp.clip(drawn, -limit, limit).astype(kind)


def setup_inputs(seed: int = 0) -> dict:
    seeds = jax.random.split(jax.random.key(seed), 6)
    return {
        "descriptors": draw_descriptors(jax.random.fold_in(seeds[5], 71), 0),
        "cell_ids": draw_cell_ids(jax.random.fold_in(seeds[5], 71), 0),
        "sub_codes": with_ends(jax.random.randint(seeds[2], (ROWS, SUB), 0, CODES), jax.random.fold_in(seeds[2], 1), 0, CODES - 1).astype(jnp.int32),
        "centroids": gaussian(seeds[3], (CELLS, D), 0.5, 3.0, ((0, 768),)),
        "codebooks": gaussian(seeds[4], (CELLS, CODES, D), 1.0, 6.0, ((0, 768),)),
    }


def newton_polar(covariance):
    norm_sq = lax.optimization_barrier(jnp.sum(covariance * covariance, axis=(-2, -1), keepdims=True))
    polar = covariance / jnp.sqrt(norm_sq + 1e-06)
    for repeat in range(NEWTON):
        gram_matrix = jnp.matmul(jnp.swapaxes(polar, -1, -2), polar, precision=lax.Precision.HIGHEST)
        polar = 1.5 * polar - 0.5 * jnp.matmul(polar, gram_matrix, precision=lax.Precision.HIGHEST)
    return polar

def reference(descriptors, cell_ids, sub_codes, centroids, codebooks):
    group_rows = ROWS_DEV * N_PEER
    group_cells = CPO * N_PEER
    capacity = N_PEER * MOST
    packed = (descriptors.reshape(N_GRP, group_rows, D), cell_ids.reshape(N_GRP, group_rows), sub_codes.reshape(N_GRP, group_rows, SUB), centroids.reshape(N_GRP, group_cells, D), codebooks.reshape(N_GRP, group_cells, CODES, D))

    def one_group(packed_group):
        rows_in, labels, codes_in, centres, books = packed_group
        onehot = (labels[:, None] == jnp.arange(group_cells, dtype=jnp.int32)[None, :]).astype(jnp.int32)
        before = jnp.cumsum(onehot, axis=0) - onehot
        within = lax.optimization_barrier(jnp.sum(before * onehot, axis=1)).astype(jnp.int32)
        slot_index = (labels * capacity + within).astype(jnp.int32)
        residual = (rows_in.astype(jnp.float32) - centres[labels].astype(jnp.float32)).astype(jnp.bfloat16)
        residual = lax.optimization_barrier(residual)
        split_books = books.reshape(group_cells, CODES, SUB, D // SUB)
        subspaces = jnp.arange(SUB, dtype=jnp.int32)[None, :]
        rebuilt = split_books[labels[:, None], codes_in, subspaces].reshape(group_rows, D)
        res_buffer = jnp.zeros((group_cells * capacity, D), jnp.bfloat16).at[slot_index].set(residual)
        res_buffer = res_buffer.reshape(group_cells, capacity, D)
        reb_buffer = jnp.zeros((group_cells * capacity, D), jnp.bfloat16).at[slot_index].set(rebuilt)
        reb_buffer = reb_buffer.reshape(group_cells, capacity, D)
        covariance = jnp.einsum('cnd,cne->cde', res_buffer.astype(jnp.float32), reb_buffer.astype(jnp.float32), precision=lax.Precision.HIGHEST)
        rotation = newton_polar(covariance)
        rotation_bf = lax.optimization_barrier(rotation.astype(jnp.bfloat16))
        turned = jnp.einsum('cnd,cde->cne', res_buffer.astype(jnp.float32), rotation_bf.astype(jnp.float32), precision=lax.Precision.HIGHEST)
        turned_rows = turned.reshape(group_cells * capacity, D)[slot_index]
        sq_error = jnp.sum((turned_rows - rebuilt.astype(jnp.float32)) ** 2)
        return (turned_rows.astype(jnp.bfloat16), rotation, sq_error)
    turned_all, rotation_all, error_all = lax.map(one_group, packed)
    rotated = turned_all.reshape(ROWS, D)
    rotations = rotation_all.reshape(CELLS, D, D)
    distortion = jnp.sum(error_all) / jnp.float32(ROWS * D)
    return (rotated, rotations, distortion)
```

```python
import jax
import jax.numpy as jnp
from jax import lax
from jax.experimental import pallas as pl
from jax.experimental.pallas import tpu as pltpu
from jax.sharding import PartitionSpec as P

MESH = pl.DeviceIdType.MESH
NEWTON = 3
D = 256
SUB = 32
CODES = 256
ROWS_DEV = 256
SLOT = 16
CODE_ROW = 10
X_SIZE, Y_SIZE = 4, 8
PEERS = X_SIZE * Y_SIZE
CHUNK = 8
CHUNKS = PEERS // CHUNK
CROWS = CHUNK * SLOT
F32, BF16, I32 = jnp.float32, jnp.bfloat16, jnp.int32


def nn(a, b):
    return jnp.dot(a, b, preferred_element_type=F32)


def nt(a, b):
    return lax.dot_general(a, b, (((1,), (1,)), ((), ())), preferred_element_type=F32)


def iota(shape, dim):
    return lax.broadcasted_iota(I32, shape, dim)


def kernel(
    groups,
    desc_ref,
    cell_ref,
    code_ref,
    cent_ref,
    book_ref,
    rotated_ref,
    rot_ref,
    dist_ref,
    send,
    got,
    back,
    ret,
    table,
    rebuilt,
    resid,
    cov,
    perm_t,
    err_mine,
    err_peer,
    err_sum,
    err_grp,
    out_sem,
    in_sem,
    back_sem,
    ret_sem,
    ep_out,
    ep_in,
    eg_out,
    eg_in,
):
    me_g = lax.axis_index("grp")
    me_p = lax.axis_index("peer")
    my_y, my_x = me_p // X_SIZE, me_p % X_SIZE

    def ahead(delta):
        to_y = (my_y + delta // X_SIZE) % Y_SIZE
        to_x = (my_x + delta % X_SIZE) % X_SIZE
        return (me_g, to_y * X_SIZE + to_x)

    def behind(delta):
        to_y = (my_y + Y_SIZE - delta // X_SIZE) % Y_SIZE
        to_x = (my_x + X_SIZE - delta % X_SIZE) % X_SIZE
        return (me_g, to_y * X_SIZE + to_x)

    def level(step):
        return ((me_g + step) % groups, me_p)

    barrier = pltpu.get_barrier_semaphore()

    def greet_peer(delta, carry):
        pl.semaphore_signal(barrier, inc=1, device_id=ahead(delta), device_id_type=MESH)
        return carry

    def greet_level(step, carry):
        pl.semaphore_signal(barrier, inc=1, device_id=level(step), device_id_type=MESH)
        return carry

    lax.fori_loop(1, PEERS, greet_peer, 0)
    lax.fori_loop(1, groups, greet_level, 0)

    cell = cell_ref[...]
    owner = cell >> 1
    rel = (((owner >> 2) - my_y) & (Y_SIZE - 1)) * X_SIZE + (((owner & 3) - my_x) & (X_SIZE - 1))
    hot = iota((PEERS, ROWS_DEV), 0) == rel
    earlier = (iota((ROWS_DEV, ROWS_DEV), 0) < iota((ROWS_DEV, ROWS_DEV), 1)).astype(F32).astype(BF16)
    count = nn(hot.astype(F32).astype(BF16), earlier)
    rank = jnp.sum(jnp.where(hot, count, 0.0), axis=0, keepdims=True).astype(I32)
    slot = rel * SLOT + rank
    code_slot = rel * SLOT + CODE_ROW + (rank >> 3)
    position = iota((PEERS * SLOT, ROWS_DEV), 0)
    place = (position == slot).astype(F32).astype(BF16)
    code_place = (position == code_slot).astype(F32).astype(BF16)
    code = code_ref[...] + 1
    signed = jnp.where((cell & 1) == 1, -code, code).astype(F32)
    spread = jnp.concatenate(
        [jnp.where((rank & 7) == k, signed, 0.0) for k in range(8)], axis=0
    ).astype(BF16)
    packed = nn(place, desc_ref[...]) + nt(code_place, spread)
    send[...] = packed.astype(BF16).reshape(PEERS, SLOT, D)

    pl.semaphore_wait(barrier, PEERS - 1 + groups - 1)

    def out_copy(delta):
        return pltpu.make_async_remote_copy(
            src_ref=send.at[delta],
            dst_ref=got.at[delta],
            send_sem=out_sem.at[delta],
            recv_sem=in_sem.at[delta],
            device_id=ahead(delta),
            device_id_type=MESH,
        )

    def start_out(delta, carry):
        out_copy(delta).start()
        return carry

    lax.fori_loop(1, PEERS, start_out, 0)
    got[0] = send[0]

    for c in range(2):
        table[c] = book_ref[c].astype(F32).T
    perm_t[...] = place.astype(F32).T.astype(BF16)
    cov[...] = jnp.zeros_like(cov)
    cent = cent_ref[...].astype(F32)

    row = iota((CROWS, CROWS), 0)
    col = iota((CROWS, CROWS), 1)
    used = (row % SLOT) < CODE_ROW
    pick = (
        (row // SLOT == col // SLOT)
        & (col % SLOT == CODE_ROW + (row % SLOT) // 8)
        & used
    ).astype(F32).astype(BF16)
    lane = iota((CROWS, D), 1)
    own_lane = (lane // SUB) == (iota((CROWS, D), 0) % SLOT) % 8
    fold = (iota((SUB, D), 1) % SUB == iota((SUB, D), 0)).astype(F32).astype(BF16)
    first = (iota((D, 128), 0) % SUB == 0).astype(F32).astype(BF16)

    def wait_in(delta, carry):
        out_copy(delta).wait_recv()
        return carry

    def decode(chunk, carry):
        lax.fori_loop(jnp.maximum(chunk * CHUNK, 1), chunk * CHUNK + CHUNK, wait_in, 0)
        rows = got[pl.ds(chunk * CHUNK, CHUNK)].reshape(CROWS, D)
        codes = jnp.where(own_lane, nn(pick, rows), 0.0).astype(BF16)
        code_t = nt(fold, codes)
        code_col = nn(codes, first)
        rows = rows.astype(F32)
        keep = [code_col > 0.0, code_col < 0.0]
        which = (jnp.abs(code_t) - 1.0).astype(I32)
        parts = [[], []]
        for s in range(SUB):
            index = jnp.broadcast_to(which[s : s + 1], (8, CROWS))
            sign = jnp.broadcast_to(code_t[s : s + 1], (8, CROWS))
            near = index & 127
            for c in range(2):
                low = table[c, 8 * s : 8 * s + 8, 0:128]
                high = table[c, 8 * s : 8 * s + 8, 128:256]
                low = jnp.take_along_axis(low, near, axis=1, mode="promise_in_bounds")
                high = jnp.take_along_axis(high, near, axis=1, mode="promise_in_bounds")
                value = jnp.where(index < 128, low, high)
                valid = sign > 0.0 if c == 0 else sign < 0.0
                parts[c].append(jnp.where(valid, value, 0.0))
        rebuilt_t = [jnp.concatenate(p, axis=0) for p in parts]
        rebuilt[chunk] = (rebuilt_t[0] + rebuilt_t[1]).T
        for c in range(2):
            residual = (rows - cent[c : c + 1]).astype(BF16)
            cov[c] += nn(rebuilt_t[c].astype(BF16), residual)
            both = jnp.concatenate([keep[c], keep[c]], axis=1)
            resid[c, chunk] = jnp.where(both, residual.astype(F32), 0.0).astype(BF16)
        return carry

    lax.fori_loop(0, CHUNKS, decode, 0)

    polar = []
    for c in range(2):
        norm = jnp.sum(cov[c] * cov[c], keepdims=True)
        polar.append(cov[c] * lax.rsqrt(norm + 1e-06))
    for _ in range(NEWTON):
        small = [q.astype(BF16) for q in polar]
        gram = [nt(q, q).astype(BF16) for q in small]
        polar = [1.5 * q - 0.5 * nn(g, b) for q, g, b in zip(polar, gram, small)]
    turn = [q.astype(BF16) for q in polar]

    def turn_chunk(chunk, total):
        turned = nt(resid[0, chunk], turn[0]) + nt(resid[1, chunk], turn[1])
        off = turned - rebuilt[chunk]
        back[pl.ds(chunk * CHUNK, CHUNK)] = turned.astype(BF16).reshape(CHUNK, SLOT, D)
        return total + jnp.sum(off * off, axis=0, keepdims=True)

    total = jnp.zeros((1, D), F32)
    for chunk in range(CHUNKS):
        total = turn_chunk(chunk, total)
    err_mine[...] = total[:, :128] + total[:, 128:]
    err_peer[0] = err_mine[...]

    def err_copy(delta):
        return pltpu.make_async_remote_copy(
            src_ref=err_mine,
            dst_ref=err_peer.at[delta],
            send_sem=ep_out.at[delta],
            recv_sem=ep_in.at[delta],
            device_id=ahead(delta),
            device_id_type=MESH,
        )

    def back_copy(delta):
        return pltpu.make_async_remote_copy(
            src_ref=back.at[delta],
            dst_ref=ret.at[delta],
            send_sem=back_sem.at[delta],
            recv_sem=ret_sem.at[delta],
            device_id=behind(delta),
            device_id_type=MESH,
        )

    def grp_copy(step):
        return pltpu.make_async_remote_copy(
            src_ref=err_sum,
            dst_ref=err_grp.at[step],
            send_sem=eg_out.at[step],
            recv_sem=eg_in.at[step],
            device_id=level(step),
            device_id_type=MESH,
        )

    def loop(stop, act):
        def body(index, carry):
            act(index)
            return carry

        lax.fori_loop(1, stop, body, 0)

    loop(PEERS, lambda d: err_copy(d).start())
    loop(PEERS, lambda d: back_copy(d).start())
    ret[0] = back[0]
    for c in range(2):
        rot_ref[c] = polar[c].T

    loop(PEERS, lambda d: err_copy(d).wait_recv())
    err_sum[...] = jnp.sum(err_peer[...], axis=0)
    err_grp[0] = err_sum[...]
    loop(groups, lambda s: grp_copy(s).start())

    loop(PEERS, lambda d: back_copy(d).wait_recv())
    rotated_ref[...] = nn(perm_t[...], ret[...].reshape(PEERS * SLOT, D)).astype(BF16)

    loop(groups, lambda s: grp_copy(s).wait_recv())
    sums = jnp.sum(err_grp[...], axis=0)
    scale = 1.0 / (ROWS_DEV * PEERS * groups * D)
    dist_ref[...] = jnp.sum(sums, axis=1, keepdims=True) * scale

    loop(PEERS, lambda d: out_copy(d).wait_send())
    loop(PEERS, lambda d: err_copy(d).wait_send())
    loop(PEERS, lambda d: back_copy(d).wait_send())
    loop(groups, lambda s: grp_copy(s).wait_send())


def solution(mesh):
    groups = mesh.shape["grp"]

    def local(descriptors, cell_ids, sub_codes, centroids, codebooks):
        rotated, rotations, distortion = pl.pallas_call(
            lambda *refs: kernel(groups, *refs),
            out_shape=(
                jax.ShapeDtypeStruct((ROWS_DEV, D), BF16),
                jax.ShapeDtypeStruct((2, D, D), F32),
                jax.ShapeDtypeStruct((1, 1), F32),
            ),
            in_specs=[pl.BlockSpec(memory_space=pltpu.VMEM)] * 5,
            out_specs=(pl.BlockSpec(memory_space=pltpu.VMEM),) * 3,
            scratch_shapes=[
                pltpu.VMEM((PEERS, SLOT, D), BF16),
                pltpu.VMEM((PEERS, SLOT, D), BF16),
                pltpu.VMEM((PEERS, SLOT, D), BF16),
                pltpu.VMEM((PEERS, SLOT, D), BF16),
                pltpu.VMEM((2, D, CODES), F32),
                pltpu.VMEM((CHUNKS, CROWS, D), F32),
                pltpu.VMEM((2, CHUNKS, CROWS, D), BF16),
                pltpu.VMEM((2, D, D), F32),
                pltpu.VMEM((ROWS_DEV, PEERS * SLOT), BF16),
                pltpu.VMEM((1, 128), F32),
                pltpu.VMEM((PEERS, 1, 128), F32),
                pltpu.VMEM((1, 128), F32),
                pltpu.VMEM((groups, 1, 128), F32),
                pltpu.SemaphoreType.DMA((PEERS,)),
                pltpu.SemaphoreType.DMA((PEERS,)),
                pltpu.SemaphoreType.DMA((PEERS,)),
                pltpu.SemaphoreType.DMA((PEERS,)),
                pltpu.SemaphoreType.DMA((PEERS,)),
                pltpu.SemaphoreType.DMA((PEERS,)),
                pltpu.SemaphoreType.DMA((groups,)),
                pltpu.SemaphoreType.DMA((groups,)),
            ],
            compiler_params=pltpu.CompilerParams(
                collective_id=0, has_side_effects=True, vmem_limit_bytes=32 * 1024 * 1024
            ),
        )(descriptors, cell_ids.reshape(1, ROWS_DEV), sub_codes.T, centroids, codebooks)
        return rotated, rotations, distortion.reshape(())

    rows = P(("grp", "peer"), None)
    cells = P(("grp", "peer"), None, None)
    return jax.shard_map(
        local,
        mesh=mesh,
        in_specs=(rows, P(("grp", "peer")), rows, rows, cells),
        out_specs=(rows, cells, P()),
        check_vma=False,
    )
```

```python
import jax
import jax.numpy as jnp
from jax import lax
from jax.experimental import pallas as pl
from jax.experimental.pallas import tpu as pltpu
from jax.sharding import PartitionSpec as P

MESH = pl.DeviceIdType.MESH
NEWTON = 3
D = 256
HALF = 128
SUB = 32
CODES = 256
ROWS_DEV = 256
OWN = 10
X_SIZE, Y_SIZE = 4, 8
PEERS = X_SIZE * Y_SIZE
MSG = 24
SLOT = 16
CHUNK = 8
CHUNKS = PEERS // CHUNK
CROWS = CHUNK * SLOT
CMSG = CHUNK * MSG
F32, BF16, I32 = jnp.float32, jnp.bfloat16, jnp.int32


def hops(delta):
    y, x = delta // X_SIZE, delta % X_SIZE
    return min(y, Y_SIZE - y) + min(x, X_SIZE - x)


FAR_FIRST = sorted(range(1, PEERS), key=lambda delta: -hops(delta))
CHUNK_ORDER = (2, 1, 3, 0)


def nn(a, b):
    return jnp.dot(a, b, preferred_element_type=F32)


def nt(a, b):
    return lax.dot_general(a, b, (((1,), (1,)), ((), ())), preferred_element_type=F32)


def iota(shape, dim):
    return lax.broadcasted_iota(I32, shape, dim)


def hot(mask):
    return mask.astype(F32).astype(BF16)


def loop(start, stop, act):
    def body(index, carry):
        act(index)
        return carry

    lax.fori_loop(start, stop, body, 0)


def kernel(
    groups,
    desc_hbm,
    cell_hbm,
    code_hbm,
    cent_hbm,
    book_hbm,
    rotated_ref,
    rot_ref,
    dist_ref,
    desc_ref,
    cell_ref,
    code_ref,
    cent_ref,
    book_ref,
    load_sem,
    send,
    got,
    back,
    ret,
    table,
    rebuilt,
    resid,
    cov,
    perm_t,
    err_mine,
    err_grp,
    err_sum,
    err_peer,
    out_sem,
    in_sem,
    back_sem,
    ret_sem,
    eg_out,
    eg_in,
    ep_out,
    ep_in,
):
    me_g = lax.axis_index("grp")
    me_p = lax.axis_index("peer")
    my_y, my_x = me_p // X_SIZE, me_p % X_SIZE
    levels = sorted(range(1, groups), key=lambda step: abs(2 * step - groups))

    def ahead(delta):
        to_y = (my_y + delta // X_SIZE) % Y_SIZE
        to_x = (my_x + delta % X_SIZE) % X_SIZE
        return (me_g, to_y * X_SIZE + to_x)

    def behind(delta):
        to_y = (my_y + Y_SIZE - delta // X_SIZE) % Y_SIZE
        to_x = (my_x + X_SIZE - delta % X_SIZE) % X_SIZE
        return (me_g, to_y * X_SIZE + to_x)

    def level(step):
        return ((me_g + step) % groups, me_p)

    barrier = pltpu.get_barrier_semaphore()
    for delta in FAR_FIRST:
        pl.semaphore_signal(barrier, inc=1, device_id=ahead(delta), device_id_type=MESH)
    for step in levels:
        pl.semaphore_signal(barrier, inc=1, device_id=level(step), device_id_type=MESH)

    loads = [
        pltpu.make_async_copy(src, dst, load_sem.at[i])
        for i, (src, dst) in enumerate(
            [
                (cell_hbm, cell_ref),
                (code_hbm, code_ref),
                (desc_hbm, desc_ref),
                (cent_hbm, cent_ref),
                (book_hbm, book_ref),
            ]
        )
    ]
    for load in loads:
        load.start()

    loads[0].wait()
    cell = cell_ref[...]
    owner = cell >> 1
    rel = (((owner >> 2) - my_y) & (Y_SIZE - 1)) * X_SIZE + (((owner & 3) - my_x) & (X_SIZE - 1))
    owned = iota((PEERS, ROWS_DEV), 0) == rel
    earlier = hot(iota((ROWS_DEV, ROWS_DEV), 0) < iota((ROWS_DEV, ROWS_DEV), 1))
    count = nn(hot(owned), earlier)
    rank = jnp.sum(jnp.where(owned, count, 0.0), axis=0, keepdims=True).astype(I32)
    low = rel * MSG + rank
    position = iota((PEERS * MSG, ROWS_DEV), 0)
    loads[1].wait()
    code = code_ref[...] + 1
    signed = jnp.where((cell & 1) == 1, -code, code).astype(F32)
    spread = jnp.concatenate(
        [jnp.where((rank & 3) == k, signed, 0.0) for k in range(4)], axis=0
    ).astype(BF16)
    loads[2].wait()
    packed = (
        nn(hot(position == low), desc_ref[:, :HALF])
        + nn(hot(position == low + OWN), desc_ref[:, HALF:])
        + nt(hot(position == rel * MSG + 2 * OWN + (rank >> 2)), spread)
    )
    send[...] = packed.astype(BF16).reshape(PEERS, MSG, HALF)

    pl.semaphore_wait(barrier, PEERS - 1 + groups - 1)

    def out_copy(delta):
        return pltpu.make_async_remote_copy(
            src_ref=send.at[delta],
            dst_ref=got.at[delta],
            send_sem=out_sem.at[delta],
            recv_sem=in_sem.at[delta],
            device_id=ahead(delta),
            device_id_type=MESH,
        )

    for delta in FAR_FIRST:
        out_copy(delta).start()
    got[0] = send[0]

    place = rel * SLOT + rank
    place_col = jnp.broadcast_to(place.astype(F32), (8, ROWS_DEV)).T[:, :1].astype(I32)
    perm_t[...] = hot(iota((ROWS_DEV, PEERS * SLOT), 1) == place_col)
    loads[3].wait()
    loads[4].wait()
    for c in range(2):
        table[c] = book_ref[c].astype(F32).T
    cov[...] = jnp.zeros_like(cov)
    cent = cent_ref[...].astype(F32)

    row = iota((CROWS, CMSG), 0)
    source, slot = row // SLOT, row % SLOT
    col = iota((CROWS, CMSG), 1)
    col_source, col_row = col // MSG, col % MSG
    same = (source == col_source) & (slot < OWN)
    pick_low = hot(same & (col_row == slot))
    pick_high = hot(same & (col_row == slot + OWN))
    pick_code = hot(same & (col_row == 2 * OWN + (slot >> 2)))
    own_lane = (iota((CROWS, HALF), 1) // SUB) == (iota((CROWS, HALF), 0) % SLOT) % 4
    fold = hot(iota((SUB, HALF), 1) % SUB == iota((SUB, HALF), 0))
    first = hot(iota((HALF, HALF), 0) % SUB == 0)

    def decode(chunk):
        loop(max(chunk * CHUNK, 1), chunk * CHUNK + CHUNK, lambda d: out_copy(d).wait_recv())
        message = got[chunk * CHUNK : chunk * CHUNK + CHUNK].reshape(CMSG, HALF)
        codes = jnp.where(own_lane, nn(pick_code, message), 0.0).astype(BF16)
        rows = jnp.concatenate([nn(pick_low, message), nn(pick_high, message)], axis=1)
        code_t = nt(fold, codes)
        code_col = nn(codes, first)
        keep = [code_col > 0.0, code_col < 0.0]
        which = (jnp.abs(code_t) - 1.0).astype(I32)
        parts = [[], []]
        for s in range(SUB):
            index = jnp.broadcast_to(which[s : s + 1], (8, CROWS))
            sign = jnp.broadcast_to(code_t[s : s + 1], (8, CROWS))
            near = index & 127
            for c in range(2):
                left = table[c, 8 * s : 8 * s + 8, 0:128]
                right = table[c, 8 * s : 8 * s + 8, 128:256]
                left = jnp.take_along_axis(left, near, axis=1, mode="promise_in_bounds")
                right = jnp.take_along_axis(right, near, axis=1, mode="promise_in_bounds")
                value = jnp.where(index < 128, left, right)
                valid = sign > 0.0 if c == 0 else sign < 0.0
                parts[c].append(jnp.where(valid, value, 0.0))
        rebuilt_t = [jnp.concatenate(p, axis=0) for p in parts]
        rebuilt[chunk] = (rebuilt_t[0] + rebuilt_t[1]).T
        for c in range(2):
            residual = (rows - cent[c : c + 1]).astype(BF16)
            cov[c] += nn(rebuilt_t[c].astype(BF16), residual)
            both = jnp.concatenate([keep[c], keep[c]], axis=1)
            resid[c, chunk] = jnp.where(both, residual.astype(F32), 0.0).astype(BF16)

    for chunk in CHUNK_ORDER:
        decode(chunk)

    polar = []
    for c in range(2):
        norm = jnp.sum(cov[c] * cov[c], keepdims=True)
        polar.append(cov[c] * lax.rsqrt(norm + 1e-06))
    for _ in range(NEWTON):
        small = [q.astype(BF16) for q in polar]
        gram = [nt(q, q).astype(BF16) for q in small]
        polar = [1.5 * q - 0.5 * nn(g, b) for q, g, b in zip(polar, gram, small)]
    turn = [q.astype(BF16) for q in polar]

    total = jnp.zeros((1, D), F32)
    for chunk in range(CHUNKS):
        turned = nt(resid[0, chunk], turn[0]) + nt(resid[1, chunk], turn[1])
        off = turned - rebuilt[chunk]
        back[chunk * CHUNK : chunk * CHUNK + CHUNK] = turned.astype(BF16).reshape(CHUNK, SLOT, D)
        total = total + jnp.sum(off * off, axis=0, keepdims=True)
    err_mine[...] = total[:, :HALF] + total[:, HALF:]

    def grp_copy(step):
        return pltpu.make_async_remote_copy(
            src_ref=err_mine,
            dst_ref=err_grp.at[step],
            send_sem=eg_out.at[step],
            recv_sem=eg_in.at[step],
            device_id=level(step),
            device_id_type=MESH,
        )

    def back_copy(delta):
        return pltpu.make_async_remote_copy(
            src_ref=back.at[delta],
            dst_ref=ret.at[delta],
            send_sem=back_sem.at[delta],
            recv_sem=ret_sem.at[delta],
            device_id=behind(delta),
            device_id_type=MESH,
        )

    def peer_copy(delta):
        return pltpu.make_async_remote_copy(
            src_ref=err_sum,
            dst_ref=err_peer.at[delta],
            send_sem=ep_out.at[delta],
            recv_sem=ep_in.at[delta],
            device_id=ahead(delta),
            device_id_type=MESH,
        )

    for step in levels:
        grp_copy(step).start()
    for delta in FAR_FIRST:
        back_copy(delta).start()
    err_grp[0] = err_mine[...]
    ret[0] = back[0]
    for c in range(2):
        rot_ref[c] = polar[c].T

    loop(1, groups, lambda s: grp_copy(s).wait_recv())
    err_sum[...] = jnp.sum(err_grp[...], axis=0)
    for delta in FAR_FIRST:
        peer_copy(delta).start()
    err_peer[0] = err_sum[...]

    loop(1, PEERS, lambda d: back_copy(d).wait_recv())
    rotated_ref[...] = nn(perm_t[...], ret[...].reshape(PEERS * SLOT, D)).astype(BF16)

    loop(1, PEERS, lambda d: out_copy(d).wait_send())
    loop(1, PEERS, lambda d: back_copy(d).wait_send())
    loop(1, groups, lambda s: grp_copy(s).wait_send())
    loop(1, PEERS, lambda d: peer_copy(d).wait_recv())
    sums = jnp.sum(err_peer[...], axis=0)
    scale = 1.0 / (ROWS_DEV * PEERS * groups * D)
    dist_ref[...] = jnp.sum(sums, axis=1, keepdims=True) * scale
    loop(1, PEERS, lambda d: peer_copy(d).wait_send())


def solution(mesh):
    groups = mesh.shape["grp"]
    vmem = pl.BlockSpec(memory_space=pltpu.VMEM)
    hbm = pl.BlockSpec(memory_space=pltpu.HBM)

    def local(descriptors, cell_ids, sub_codes, centroids, codebooks):
        operands = (
            descriptors,
            cell_ids.reshape(1, ROWS_DEV),
            sub_codes.T,
            centroids,
            codebooks,
        )
        rotated, rotations, distortion = pl.pallas_call(
            lambda *refs: kernel(groups, *refs),
            out_shape=(
                pltpu.VMEM((ROWS_DEV, D), BF16),
                pltpu.VMEM((2, D, D), F32),
                jax.ShapeDtypeStruct((1, 1), F32),
            ),
            in_specs=[hbm] * 5,
            out_specs=(vmem,) * 3,
            scratch_shapes=[
                pltpu.VMEM((ROWS_DEV, D), BF16),
                pltpu.VMEM((1, ROWS_DEV), I32),
                pltpu.VMEM((SUB, ROWS_DEV), I32),
                pltpu.VMEM((2, D), BF16),
                pltpu.VMEM((2, CODES, D), BF16),
                pltpu.SemaphoreType.DMA((5,)),
                pltpu.VMEM((PEERS, MSG, HALF), BF16),
                pltpu.VMEM((PEERS, MSG, HALF), BF16),
                pltpu.VMEM((PEERS, SLOT, D), BF16),
                pltpu.VMEM((PEERS, SLOT, D), BF16),
                pltpu.VMEM((2, D, CODES), F32),
                pltpu.VMEM((CHUNKS, CROWS, D), F32),
                pltpu.VMEM((2, CHUNKS, CROWS, D), BF16),
                pltpu.VMEM((2, D, D), F32),
                pltpu.VMEM((ROWS_DEV, PEERS * SLOT), BF16),
                pltpu.VMEM((1, HALF), F32),
                pltpu.VMEM((groups, 1, HALF), F32),
                pltpu.VMEM((1, HALF), F32),
                pltpu.VMEM((PEERS, 1, HALF), F32),
                pltpu.SemaphoreType.DMA((PEERS,)),
                pltpu.SemaphoreType.DMA((PEERS,)),
                pltpu.SemaphoreType.DMA((PEERS,)),
                pltpu.SemaphoreType.DMA((PEERS,)),
                pltpu.SemaphoreType.DMA((groups,)),
                pltpu.SemaphoreType.DMA((groups,)),
                pltpu.SemaphoreType.DMA((PEERS,)),
                pltpu.SemaphoreType.DMA((PEERS,)),
            ],
            compiler_params=pltpu.CompilerParams(
                collective_id=0, has_side_effects=True, vmem_limit_bytes=32 * 1024 * 1024
            ),
        )(*(pltpu.with_memory_space_constraint(x, pltpu.HBM) for x in operands))
        return rotated, rotations, distortion.reshape(())

    rows = P(("grp", "peer"), None)
    cells = P(("grp", "peer"), None, None)
    return jax.shard_map(
        local,
        mesh=mesh,
        in_specs=(rows, P(("grp", "peer")), rows, rows, cells),
        out_specs=(rows, cells, P()),
        check_vma=False,
    )
```

```python
import jax
import jax.numpy as jnp
from jax import lax
from jax.experimental import pallas as pl
from jax.experimental.pallas import tpu as pltpu
from jax.sharding import PartitionSpec as P

MESH = pl.DeviceIdType.MESH
NEWTON = 3
D = 256
HALF = 128
SUB = 32
CODES = 256
ROWS_DEV = 256
OWN = 10
X_SIZE, Y_SIZE = 4, 8
PEERS = X_SIZE * Y_SIZE
MSG = 24
SLOT = 16
CHUNK = 8
CHUNKS = PEERS // CHUNK
CROWS = CHUNK * SLOT
CMSG = CHUNK * MSG
F32, BF16, I32 = jnp.float32, jnp.bfloat16, jnp.int32


def hops(delta):
    y, x = delta // X_SIZE, delta % X_SIZE
    return min(y, Y_SIZE - y) + min(x, X_SIZE - x)


FAR_FIRST = sorted(range(1, PEERS), key=lambda delta: -hops(delta))
CHUNK_ORDER = (2, 1, 3, 0)


def nn(a, b):
    return jnp.dot(a, b, preferred_element_type=F32)


def nt(a, b):
    return lax.dot_general(a, b, (((1,), (1,)), ((), ())), preferred_element_type=F32)


def iota(shape, dim):
    return lax.broadcasted_iota(I32, shape, dim)


def hot(mask):
    return mask.astype(F32).astype(BF16)


def drain(ref, sem):
    pltpu.make_async_copy(ref, ref, sem.at[0]).wait()


def kernel(
    groups,
    desc_hbm,
    cell_hbm,
    code_hbm,
    cent_hbm,
    book_hbm,
    rotated_ref,
    rot_ref,
    dist_ref,
    desc_ref,
    cell_ref,
    code_ref,
    cent_ref,
    book_ref,
    load_sem,
    send,
    got,
    back,
    ret,
    table,
    rebuilt,
    resid,
    decoded,
    perm_t,
    err_mine,
    err_grp,
    err_sum,
    err_peer,
    out_sem,
    in_sem,
    back_sem,
    ret_sem,
    eg_out,
    eg_in,
    ep_out,
    ep_in,
):
    me_g = lax.axis_index("grp")
    me_p = lax.axis_index("peer")
    my_y, my_x = me_p // X_SIZE, me_p % X_SIZE
    levels = sorted(range(1, groups), key=lambda step: abs(2 * step - groups))

    def ahead(delta):
        to_y = (my_y + delta // X_SIZE) % Y_SIZE
        to_x = (my_x + delta % X_SIZE) % X_SIZE
        return (me_g, to_y * X_SIZE + to_x)

    def behind(delta):
        to_y = (my_y + Y_SIZE - delta // X_SIZE) % Y_SIZE
        to_x = (my_x + X_SIZE - delta % X_SIZE) % X_SIZE
        return (me_g, to_y * X_SIZE + to_x)

    def level(step):
        return ((me_g + step) % groups, me_p)

    loads = [
        pltpu.make_async_copy(src, dst, load_sem.at[i])
        for i, (src, dst) in enumerate(
            [
                (cell_hbm, cell_ref),
                (code_hbm, code_ref),
                (desc_hbm, desc_ref),
                (cent_hbm, cent_ref),
                (book_hbm, book_ref),
            ]
        )
    ]
    for load in loads:
        load.start()

    barrier = pltpu.get_barrier_semaphore()
    for delta in FAR_FIRST:
        pl.semaphore_signal(barrier, inc=1, device_id=ahead(delta), device_id_type=MESH)
    for step in levels:
        pl.semaphore_signal(barrier, inc=1, device_id=level(step), device_id_type=MESH)

    loads[0].wait()
    cell = cell_ref[...]
    owner = cell >> 1
    rel = (((owner >> 2) - my_y) & (Y_SIZE - 1)) * X_SIZE + (((owner & 3) - my_x) & (X_SIZE - 1))
    owned = iota((PEERS, ROWS_DEV), 0) == rel
    earlier = hot(iota((ROWS_DEV, ROWS_DEV), 0) < iota((ROWS_DEV, ROWS_DEV), 1))
    count = nn(hot(owned), earlier)
    rank = jnp.sum(jnp.where(owned, count, 0.0), axis=0, keepdims=True).astype(I32)
    low = rel * MSG + rank
    position = iota((PEERS * MSG, ROWS_DEV), 0)
    loads[1].wait()
    code = code_ref[...] + 1
    signed = jnp.where((cell & 1) == 1, -code, code).astype(F32)
    spread = jnp.concatenate(
        [jnp.where((rank & 3) == k, signed, 0.0) for k in range(4)], axis=0
    ).astype(BF16)
    loads[2].wait()
    packed = (
        nn(hot(position == low), desc_ref[:, :HALF])
        + nn(hot(position == low + OWN), desc_ref[:, HALF:])
        + nt(hot(position == rel * MSG + 2 * OWN + (rank >> 2)), spread)
    )
    send[...] = packed.astype(BF16).reshape(PEERS, MSG, HALF)

    pl.semaphore_wait(barrier, PEERS - 1 + groups - 1)

    def out_copy(delta):
        return pltpu.make_async_remote_copy(
            src_ref=send.at[delta],
            dst_ref=got.at[delta],
            send_sem=out_sem.at[0],
            recv_sem=in_sem.at[delta // CHUNK],
            device_id=ahead(delta),
            device_id_type=MESH,
        )

    for delta in FAR_FIRST:
        out_copy(delta).start()
    got[0] = send[0]

    place = rel * SLOT + rank
    place_col = jnp.broadcast_to(place.astype(F32), (8, ROWS_DEV)).T[:, :1].astype(I32)
    perm_t[...] = hot(iota((ROWS_DEV, PEERS * SLOT), 1) == place_col)
    loads[3].wait()
    loads[4].wait()
    for c in range(2):
        table[c] = book_ref[c].astype(F32).T
    cent = cent_ref[...].astype(F32)

    row = iota((CROWS, CMSG), 0)
    source, slot = row // SLOT, row % SLOT
    col = iota((CROWS, CMSG), 1)
    col_source, col_row = col // MSG, col % MSG
    same = (source == col_source) & (slot < OWN)
    pick_low = hot(same & (col_row == slot))
    pick_high = hot(same & (col_row == slot + OWN))
    pick_code = hot(same & (col_row == 2 * OWN + (slot >> 2)))
    own_lane = (iota((CROWS, HALF), 1) // SUB) == (iota((CROWS, HALF), 0) % SLOT) % 4
    fold = hot(iota((SUB, HALF), 1) % SUB == iota((SUB, HALF), 0))
    first = hot(iota((HALF, HALF), 0) % SUB == 0)

    def decode(chunk):
        arrived = got.at[max(chunk * CHUNK, 1) : chunk * CHUNK + CHUNK]
        pltpu.make_async_copy(arrived, arrived, in_sem.at[chunk]).wait()
        message = got[chunk * CHUNK : chunk * CHUNK + CHUNK].reshape(CMSG, HALF)
        codes = jnp.where(own_lane, nn(pick_code, message), 0.0).astype(BF16)
        rows = jnp.concatenate([nn(pick_low, message), nn(pick_high, message)], axis=1)
        code_t = nt(fold, codes)
        code_col = nn(codes, first)
        keep = [code_col > 0.0, code_col < 0.0]
        which = (jnp.abs(code_t) - 1.0).astype(I32)
        parts = [[], []]
        for s in range(SUB):
            index = jnp.broadcast_to(which[s : s + 1], (8, CROWS))
            sign = jnp.broadcast_to(code_t[s : s + 1], (8, CROWS))
            near = index & 127
            for c in range(2):
                left = table[c, 8 * s : 8 * s + 8, 0:128]
                right = table[c, 8 * s : 8 * s + 8, 128:256]
                left = jnp.take_along_axis(left, near, axis=1, mode="promise_in_bounds")
                right = jnp.take_along_axis(right, near, axis=1, mode="promise_in_bounds")
                value = jnp.where(index < 128, left, right)
                valid = sign > 0.0 if c == 0 else sign < 0.0
                parts[c].append(jnp.where(valid, value, 0.0))
        rebuilt_t = [jnp.concatenate(p, axis=0) for p in parts]
        here = slice(chunk * CROWS, chunk * CROWS + CROWS)
        rebuilt[here] = (rebuilt_t[0] + rebuilt_t[1]).T
        for c in range(2):
            both = jnp.concatenate([keep[c], keep[c]], axis=1)
            resid[c, here] = jnp.where(both, rows - cent[c : c + 1], 0.0).astype(BF16)
            decoded[c, :, here] = rebuilt_t[c].astype(BF16)

    for chunk in CHUNK_ORDER:
        decode(chunk)

    cov = [nn(decoded[c], resid[c]) for c in range(2)]
    inverse = [lax.rsqrt(jnp.sum(m * m, keepdims=True) + 1e-06) for m in cov]
    small = [m.astype(BF16) for m in cov]
    gram = [(nt(b, b) * (i * i)).astype(BF16) for b, i in zip(small, inverse)]
    polar = [i * (1.5 * m - 0.5 * nn(g, b)) for m, g, b, i in zip(cov, gram, small, inverse)]
    for _ in range(NEWTON - 1):
        small = [q.astype(BF16) for q in polar]
        gram = [nt(b, b).astype(BF16) for b in small]
        polar = [1.5 * q - 0.5 * nn(g, b) for q, g, b in zip(polar, gram, small)]
    turn = [q.astype(BF16) for q in polar]

    turned = nt(resid[0], turn[0]) + nt(resid[1], turn[1])
    back[...] = turned.astype(BF16).reshape(PEERS, SLOT, D)
    off = turned - rebuilt[...]
    total = jnp.sum(off * off, axis=0, keepdims=True)
    err_mine[...] = total[:, :HALF] + total[:, HALF:]

    def grp_copy(step):
        return pltpu.make_async_remote_copy(
            src_ref=err_mine,
            dst_ref=err_grp.at[step],
            send_sem=eg_out.at[0],
            recv_sem=eg_in.at[0],
            device_id=level(step),
            device_id_type=MESH,
        )

    def back_copy(delta):
        return pltpu.make_async_remote_copy(
            src_ref=back.at[delta],
            dst_ref=ret.at[delta],
            send_sem=back_sem.at[0],
            recv_sem=ret_sem.at[0],
            device_id=behind(delta),
            device_id_type=MESH,
        )

    def peer_copy(delta):
        return pltpu.make_async_remote_copy(
            src_ref=err_sum,
            dst_ref=err_peer.at[delta],
            send_sem=ep_out.at[0],
            recv_sem=ep_in.at[0],
            device_id=ahead(delta),
            device_id_type=MESH,
        )

    for step in levels:
        grp_copy(step).start()
    for delta in FAR_FIRST:
        back_copy(delta).start()
    err_grp[0] = err_mine[...]
    ret[0] = back[0]
    for c in range(2):
        rot_ref[c] = polar[c].T
    drain(send.at[1:PEERS], out_sem)

    drain(err_grp.at[1:groups], eg_in)
    err_sum[...] = jnp.sum(err_grp[...], axis=0)
    for delta in FAR_FIRST:
        peer_copy(delta).start()
    err_peer[0] = err_sum[...]

    drain(ret.at[1:PEERS], ret_sem)
    rotated_ref[...] = nn(perm_t[...], ret[...].reshape(PEERS * SLOT, D)).astype(BF16)

    drain(back.at[1:PEERS], back_sem)
    drain(err_grp.at[1:groups], eg_out)
    drain(err_peer.at[1:PEERS], ep_in)
    sums = jnp.sum(err_peer[...], axis=0)
    scale = 1.0 / (ROWS_DEV * PEERS * groups * D)
    dist_ref[0, 0] = jnp.sum(sums) * scale
    drain(err_peer.at[1:PEERS], ep_out)


def place_results(rotated_in, rot_in, rotated_out, rot_out, sem):
    copies = [
        pltpu.make_async_copy(rot_in, rot_out, sem.at[0]),
        pltpu.make_async_copy(rotated_in, rotated_out, sem.at[1]),
    ]
    for copy in copies:
        copy.start()
    for copy in copies:
        copy.wait()


def solution(mesh):
    groups = mesh.shape["grp"]
    vmem = pl.BlockSpec(memory_space=pltpu.VMEM)
    hbm = pl.BlockSpec(memory_space=pltpu.HBM)

    def local(descriptors, cell_ids, sub_codes, centroids, codebooks):
        operands = (
            descriptors,
            cell_ids.reshape(1, ROWS_DEV),
            sub_codes.T,
            centroids,
            codebooks,
        )
        rotated, rotations, distortion = pl.pallas_call(
            lambda *refs: kernel(groups, *refs),
            out_shape=(
                pltpu.VMEM((ROWS_DEV, D), BF16),
                pltpu.VMEM((2, D, D), F32),
                pltpu.SMEM((1, 1), F32),
            ),
            in_specs=[hbm] * 5,
            out_specs=(vmem, vmem, pl.BlockSpec(memory_space=pltpu.SMEM)),
            scratch_shapes=[
                pltpu.VMEM((ROWS_DEV, D), BF16),
                pltpu.VMEM((1, ROWS_DEV), I32),
                pltpu.VMEM((SUB, ROWS_DEV), I32),
                pltpu.VMEM((2, D), BF16),
                pltpu.VMEM((2, CODES, D), BF16),
                pltpu.SemaphoreType.DMA((5,)),
                pltpu.VMEM((PEERS, MSG, HALF), BF16),
                pltpu.VMEM((PEERS, MSG, HALF), BF16),
                pltpu.VMEM((PEERS, SLOT, D), BF16),
                pltpu.VMEM((PEERS, SLOT, D), BF16),
                pltpu.VMEM((2, D, CODES), F32),
                pltpu.VMEM((PEERS * SLOT, D), F32),
                pltpu.VMEM((2, PEERS * SLOT, D), BF16),
                pltpu.VMEM((2, D, PEERS * SLOT), BF16),
                pltpu.VMEM((ROWS_DEV, PEERS * SLOT), BF16),
                pltpu.VMEM((1, HALF), F32),
                pltpu.VMEM((groups, 1, HALF), F32),
                pltpu.VMEM((1, HALF), F32),
                pltpu.VMEM((PEERS, 1, HALF), F32),
                pltpu.SemaphoreType.DMA((1,)),
                pltpu.SemaphoreType.DMA((CHUNKS,)),
                pltpu.SemaphoreType.DMA((1,)),
                pltpu.SemaphoreType.DMA((1,)),
                pltpu.SemaphoreType.DMA((1,)),
                pltpu.SemaphoreType.DMA((1,)),
                pltpu.SemaphoreType.DMA((1,)),
                pltpu.SemaphoreType.DMA((1,)),
            ],
            compiler_params=pltpu.CompilerParams(
                collective_id=0, has_side_effects=True, vmem_limit_bytes=32 * 1024 * 1024
            ),
        )(*(pltpu.with_memory_space_constraint(x, pltpu.HBM) for x in operands))
        rotated, rotations = pl.pallas_call(
            place_results,
            out_shape=(pltpu.HBM((ROWS_DEV, D), BF16), pltpu.HBM((2, D, D), F32)),
            in_specs=[pl.BlockSpec(memory_space=pl.ANY)] * 2,
            out_specs=(hbm, hbm),
            scratch_shapes=[pltpu.SemaphoreType.DMA((2,))],
            compiler_params=pltpu.CompilerParams(vmem_limit_bytes=1024 * 1024),
        )(rotated, rotations)
        return rotated, rotations, distortion.reshape(())

    rows = P(("grp", "peer"), None)
    cells = P(("grp", "peer"), None, None)
    return jax.shard_map(
        local,
        mesh=mesh,
        in_specs=(rows, P(("grp", "peer")), rows, rows, cells),
        out_specs=(rows, cells, P()),
        check_vma=False,
    )
```

```python
import jax
import jax.numpy as jnp
from jax import lax
from jax.experimental import pallas as pl
from jax.experimental.pallas import tpu as pltpu
from jax.sharding import PartitionSpec as P

MESH = pl.DeviceIdType.MESH
NEWTON = 3
D = 256
HALF = 128
SUB = 32
CODES = 256
ROWS_DEV = 256
OWN = 10
X_SIZE, Y_SIZE = 4, 8
PEERS = X_SIZE * Y_SIZE
MSG = 24
SLOT = 16
CHUNK = 8
CHUNKS = PEERS // CHUNK
CORES = 2
HUB_PLANES = 4
CROWS = CHUNK * SLOT
CMSG = CHUNK * MSG
F32, BF16, I32 = jnp.float32, jnp.bfloat16, jnp.int32


def hops(delta):
    y, x = delta // X_SIZE, delta % X_SIZE
    return min(y, Y_SIZE - y) + min(x, X_SIZE - x)


FAR_FIRST = sorted(range(1, PEERS), key=lambda delta: -hops(delta))
CHUNK_ORDER = ((2, 1, 3, 0),)


def nn(a, b):
    return jnp.dot(a, b, preferred_element_type=F32)


def nt(a, b):
    return lax.dot_general(a, b, (((1,), (1,)), ((), ())), preferred_element_type=F32)


def iota(shape, dim):
    return lax.broadcasted_iota(I32, shape, dim)


def hot(mask):
    return mask.astype(F32).astype(BF16)


def drain(ref, sem):
    pltpu.make_async_copy(ref, ref, sem.at[0]).wait()


def kernel(
    groups,
    desc_hbm,
    cell_hbm,
    code_hbm,
    cent_hbm,
    book_hbm,
    rotated_ref,
    rot_ref,
    dist_ref,
    desc_ref,
    cell_ref,
    code_ref,
    cent_ref,
    book_ref,
    load_sem,
    send,
    got,
    back,
    ret,
    table,
    rebuilt,
    resid,
    decoded,
    perm_t,
    err_mine,
    err_grp,
    err_sum,
    err_peer,
    err_total,
    out_sem,
    in_sem,
    back_sem,
    ret_sem,
    eg_out,
    eg_in,
    ep_out,
    ep_in,
    et_out,
    et_in,
):
    me_g = lax.axis_index("grp")
    me_p = lax.axis_index("peer")
    my_y, my_x = me_p // X_SIZE, me_p % X_SIZE
    core, plane = me_g % CORES, me_g // CORES
    hubs = min(HUB_PLANES * CORES, groups)
    far = range(HUB_PLANES, groups // CORES)
    is_hub = me_g < hubs
    is_relay = plane == HUB_PLANES - 1
    greeted = PEERS - 1 + jnp.where(is_hub, hubs - 1, hubs) + jnp.where(is_relay, len(far), 0)

    def ahead(delta):
        to_y = (my_y + delta // X_SIZE) % Y_SIZE
        to_x = (my_x + delta % X_SIZE) % X_SIZE
        return (me_g, to_y * X_SIZE + to_x)

    def behind(delta):
        to_y = (my_y + Y_SIZE - delta // X_SIZE) % Y_SIZE
        to_x = (my_x + X_SIZE - delta % X_SIZE) % X_SIZE
        return (me_g, to_y * X_SIZE + to_x)

    def level(step):
        return ((me_g + step) % groups, me_p)

    loads = [
        pltpu.make_async_copy(src, dst, load_sem.at[i])
        for i, (src, dst) in enumerate(
            [
                (cell_hbm, cell_ref),
                (code_hbm, code_ref),
                (desc_hbm, desc_ref),
                (cent_hbm, cent_ref),
                (book_hbm, book_ref),
            ]
        )
    ]
    for load in loads:
        load.start()

    barrier = pltpu.get_barrier_semaphore()
    for delta in FAR_FIRST:
        pl.semaphore_signal(barrier, inc=1, device_id=ahead(delta), device_id_type=MESH)

    @pl.when(is_hub)
    def _():
        for step in range(1, groups):
            pl.semaphore_signal(barrier, inc=1, device_id=level(step), device_id_type=MESH)

    @pl.when(jnp.logical_not(is_hub))
    def _():
        relay = ((HUB_PLANES - 1) * CORES + core, me_p)
        pl.semaphore_signal(barrier, inc=1, device_id=relay, device_id_type=MESH)

    loads[0].wait()
    cell = cell_ref[...]
    owner = cell >> 1
    rel = (((owner >> 2) - my_y) & (Y_SIZE - 1)) * X_SIZE + (((owner & 3) - my_x) & (X_SIZE - 1))
    owned = iota((PEERS, ROWS_DEV), 0) == rel
    earlier = hot(iota((ROWS_DEV, ROWS_DEV), 0) < iota((ROWS_DEV, ROWS_DEV), 1))
    count = nn(hot(owned), earlier)
    rank = jnp.sum(jnp.where(owned, count, 0.0), axis=0, keepdims=True).astype(I32)
    low = rel * MSG + rank
    position = iota((PEERS * MSG, ROWS_DEV), 0)
    loads[1].wait()
    code = code_ref[...] + 1
    signed = jnp.where((cell & 1) == 1, -code, code).astype(F32)
    spread = jnp.concatenate(
        [jnp.where((rank & 3) == k, signed, 0.0) for k in range(4)], axis=0
    ).astype(BF16)
    loads[2].wait()
    packed = (
        nn(hot(position == low), desc_ref[:, :HALF])
        + nn(hot(position == low + OWN), desc_ref[:, HALF:])
        + nt(hot(position == rel * MSG + 2 * OWN + (rank >> 2)), spread)
    )
    send[...] = packed.astype(BF16).reshape(PEERS, MSG, HALF)

    pl.semaphore_wait(barrier, greeted)

    def out_copy(delta):
        return pltpu.make_async_remote_copy(
            src_ref=send.at[delta],
            dst_ref=got.at[delta],
            send_sem=out_sem.at[0],
            recv_sem=in_sem.at[delta // CHUNK],
            device_id=ahead(delta),
            device_id_type=MESH,
        )

    for delta in FAR_FIRST:
        out_copy(delta).start()
    got[0] = send[0]

    place = rel * SLOT + rank
    place_col = jnp.broadcast_to(place.astype(F32), (8, ROWS_DEV)).T[:, :1].astype(I32)
    perm_t[...] = hot(iota((ROWS_DEV, PEERS * SLOT), 1) == place_col)
    loads[3].wait()
    loads[4].wait()
    for c in range(2):
        table[c] = book_ref[c].astype(F32).T
    cent = cent_ref[...].astype(F32)

    row = iota((CROWS, CMSG), 0)
    source, slot = row // SLOT, row % SLOT
    col = iota((CROWS, CMSG), 1)
    col_source, col_row = col // MSG, col % MSG
    same = (source == col_source) & (slot < OWN)
    pick_low = hot(same & (col_row == slot))
    pick_high = hot(same & (col_row == slot + OWN))
    pick_code = hot(same & (col_row == 2 * OWN + (slot >> 2)))
    own_lane = (iota((CROWS, HALF), 1) // SUB) == (iota((CROWS, HALF), 0) % SLOT) % 4
    fold = hot(iota((SUB, HALF), 1) % SUB == iota((SUB, HALF), 0))
    first = hot(iota((HALF, HALF), 0) % SUB == 0)

    def decode(chunks):
        messages = []
        for chunk in chunks:
            arrived = got.at[max(chunk * CHUNK, 1) : chunk * CHUNK + CHUNK]
            pltpu.make_async_copy(arrived, arrived, in_sem.at[chunk]).wait()
        for chunk in chunks:
            message = got[chunk * CHUNK : chunk * CHUNK + CHUNK].reshape(CMSG, HALF)
            messages.append(message)
        codes = [jnp.where(own_lane, nn(pick_code, m), 0.0).astype(BF16) for m in messages]
        code_ts = [nt(fold, x) for x in codes]
        code_cols = [nn(x, first) for x in codes]
        for chunk, message, code_t, code_col in zip(chunks, messages, code_ts, code_cols):
            here = slice(chunk * CROWS, chunk * CROWS + CROWS)
            which = (jnp.abs(code_t) - 1.0).astype(I32)
            parts = [[], []]
            for s in range(SUB):
                index = jnp.broadcast_to(which[s : s + 1], (8, CROWS))
                sign = jnp.broadcast_to(code_t[s : s + 1], (8, CROWS))
                near = index & 127
                part = slice(8 * s, 8 * s + 8)
                values = []
                for c in range(2):
                    left = table[c, part, 0:128]
                    right = table[c, part, 128:256]
                    left = jnp.take_along_axis(left, near, axis=1, mode="promise_in_bounds")
                    right = jnp.take_along_axis(right, near, axis=1, mode="promise_in_bounds")
                    value = jnp.where(index < 128, left, right)
                    valid = sign > 0.0 if c == 0 else sign < 0.0
                    values.append(jnp.where(valid, value, 0.0))
                    parts[c].append(values[c])
            rebuilt_t = [jnp.concatenate(p, axis=0) for p in parts]
            for c in range(2):
                decoded[c, :, here] = rebuilt_t[c].astype(BF16)
            rebuilt[here] = (rebuilt_t[0] + rebuilt_t[1]).T
            rows = jnp.concatenate([nn(pick_low, message), nn(pick_high, message)], axis=1)
            keep = [code_col > 0.0, code_col < 0.0]
            for c in range(2):
                both = jnp.concatenate([keep[c], keep[c]], axis=1)
                resid[c, here] = jnp.where(both, rows - cent[c : c + 1], 0.0).astype(BF16)

    for chunks in CHUNK_ORDER:
        decode(chunks)

    cov = [nn(decoded[c], resid[c]) for c in range(2)]
    inverse = [lax.rsqrt(jnp.sum(m * m, keepdims=True) + 1e-06) for m in cov]
    small = [m.astype(BF16) for m in cov]
    gram = [(nt(b, b) * (i * i)).astype(BF16) for b, i in zip(small, inverse)]
    polar = [i * (1.5 * m - 0.5 * nn(g, b)) for m, g, b, i in zip(cov, gram, small, inverse)]
    for _ in range(NEWTON - 1):
        small = [q.astype(BF16) for q in polar]
        gram = [nt(b, b).astype(BF16) for b in small]
        polar = [1.5 * q - 0.5 * nn(g, b) for q, g, b in zip(polar, gram, small)]
    turn = [q.astype(BF16) for q in polar]

    turned = nt(resid[0], turn[0]) + nt(resid[1], turn[1])
    off = turned - rebuilt[...]
    total = jnp.sum(off * off, axis=0, keepdims=True)
    err_mine[...] = total[:, :HALF] + total[:, HALF:]

    def hub_copy(hub):
        return pltpu.make_async_remote_copy(
            src_ref=err_mine,
            dst_ref=err_grp.at[(me_g + groups - hub) % groups],
            send_sem=eg_out.at[0],
            recv_sem=eg_in.at[0],
            device_id=(hub, me_p),
            device_id_type=MESH,
        )

    def total_copy(to_plane):
        return pltpu.make_async_remote_copy(
            src_ref=err_total,
            dst_ref=err_total,
            send_sem=et_out.at[0],
            recv_sem=et_in.at[0],
            device_id=(to_plane * CORES + core, me_p),
            device_id_type=MESH,
        )

    def back_copy(delta):
        return pltpu.make_async_remote_copy(
            src_ref=back.at[delta],
            dst_ref=ret.at[delta],
            send_sem=back_sem.at[0],
            recv_sem=ret_sem.at[0],
            device_id=behind(delta),
            device_id_type=MESH,
        )

    def peer_copy(delta):
        return pltpu.make_async_remote_copy(
            src_ref=err_sum,
            dst_ref=err_peer.at[delta],
            send_sem=ep_out.at[0],
            recv_sem=ep_in.at[0],
            device_id=ahead(delta),
            device_id_type=MESH,
        )

    for hub in range(hubs):

        @pl.when(me_g != hub)
        def _():
            hub_copy(hub).start()

    back[...] = turned.astype(BF16).reshape(PEERS, SLOT, D)
    for delta in FAR_FIRST:
        back_copy(delta).start()
    err_grp[0] = err_mine[...]
    ret[0] = back[0]
    for c in range(2):
        rot_ref[c] = polar[c].T
    drain(send.at[1:PEERS], out_sem)

    @pl.when(is_hub)
    def _():
        drain(err_grp.at[1:groups], eg_in)
        err_sum[...] = jnp.sum(err_grp[...], axis=0)
        for delta in FAR_FIRST:
            peer_copy(delta).start()
        err_peer[0] = err_sum[...]
        drain(err_grp.at[1:hubs], eg_out)

    @pl.when(jnp.logical_not(is_hub))
    def _():
        drain(err_grp.at[0:hubs], eg_out)

    drain(ret.at[1:PEERS], ret_sem)
    rotated_ref[...] = nn(perm_t[...], ret[...].reshape(PEERS * SLOT, D)).astype(BF16)
    drain(back.at[1:PEERS], back_sem)

    @pl.when(is_hub)
    def _():
        drain(err_peer.at[1:PEERS], ep_in)
        err_total[...] = jnp.sum(err_peer[...], axis=0)
        drain(err_peer.at[1:PEERS], ep_out)

    if far:

        @pl.when(is_relay)
        def _():
            for to_plane in far:
                total_copy(to_plane).start()

        @pl.when(jnp.logical_not(is_hub))
        def _():
            drain(err_total, et_in)

    scale = 1.0 / (ROWS_DEV * PEERS * groups * D)
    dist_ref[0, 0] = jnp.sum(err_total[...]) * scale

    if far:

        @pl.when(is_relay)
        def _():
            drain(err_grp.at[0 : len(far)], et_out)


def place_results(rotated_in, rot_in, rotated_out, rot_out, sem):
    copies = [
        pltpu.make_async_copy(rot_in, rot_out, sem.at[0]),
        pltpu.make_async_copy(rotated_in, rotated_out, sem.at[1]),
    ]
    for copy in copies:
        copy.start()
    for copy in copies:
        copy.wait()


def solution(mesh):
    groups = mesh.shape["grp"]
    vmem = pl.BlockSpec(memory_space=pltpu.VMEM)
    hbm = pl.BlockSpec(memory_space=pltpu.HBM)

    def local(descriptors, cell_ids, sub_codes, centroids, codebooks):
        operands = (
            descriptors,
            cell_ids.reshape(1, ROWS_DEV),
            sub_codes.T,
            centroids,
            codebooks,
        )
        rotated, rotations, distortion = pl.pallas_call(
            lambda *refs: kernel(groups, *refs),
            out_shape=(
                pltpu.VMEM((ROWS_DEV, D), BF16),
                pltpu.VMEM((2, D, D), F32),
                pltpu.SMEM((1, 1), F32),
            ),
            in_specs=[hbm] * 5,
            out_specs=(vmem, vmem, pl.BlockSpec(memory_space=pltpu.SMEM)),
            scratch_shapes=[
                pltpu.VMEM((ROWS_DEV, D), BF16),
                pltpu.VMEM((1, ROWS_DEV), I32),
                pltpu.VMEM((SUB, ROWS_DEV), I32),
                pltpu.VMEM((2, D), BF16),
                pltpu.VMEM((2, CODES, D), BF16),
                pltpu.SemaphoreType.DMA((5,)),
                pltpu.VMEM((PEERS, MSG, HALF), BF16),
                pltpu.VMEM((PEERS, MSG, HALF), BF16),
                pltpu.VMEM((PEERS, SLOT, D), BF16),
                pltpu.VMEM((PEERS, SLOT, D), BF16),
                pltpu.VMEM((2, D, CODES), F32),
                pltpu.VMEM((PEERS * SLOT, D), F32),
                pltpu.VMEM((2, PEERS * SLOT, D), BF16),
                pltpu.VMEM((2, D, PEERS * SLOT), BF16),
                pltpu.VMEM((ROWS_DEV, PEERS * SLOT), BF16),
                pltpu.VMEM((1, HALF), F32),
                pltpu.VMEM((groups, 1, HALF), F32),
                pltpu.VMEM((1, HALF), F32),
                pltpu.VMEM((PEERS, 1, HALF), F32),
                pltpu.VMEM((1, HALF), F32),
                pltpu.SemaphoreType.DMA((1,)),
                pltpu.SemaphoreType.DMA((CHUNKS,)),
                pltpu.SemaphoreType.DMA((1,)),
                pltpu.SemaphoreType.DMA((1,)),
                pltpu.SemaphoreType.DMA((1,)),
                pltpu.SemaphoreType.DMA((1,)),
                pltpu.SemaphoreType.DMA((1,)),
                pltpu.SemaphoreType.DMA((1,)),
                pltpu.SemaphoreType.DMA((1,)),
                pltpu.SemaphoreType.DMA((1,)),
            ],
            compiler_params=pltpu.CompilerParams(
                collective_id=0, has_side_effects=True, vmem_limit_bytes=32 * 1024 * 1024
            ),
        )(*(pltpu.with_memory_space_constraint(x, pltpu.HBM) for x in operands))
        rotated, rotations = pl.pallas_call(
            place_results,
            out_shape=(pltpu.HBM((ROWS_DEV, D), BF16), pltpu.HBM((2, D, D), F32)),
            in_specs=[pl.BlockSpec(memory_space=pl.ANY)] * 2,
            out_specs=(hbm, hbm),
            scratch_shapes=[pltpu.SemaphoreType.DMA((2,))],
            compiler_params=pltpu.CompilerParams(vmem_limit_bytes=1024 * 1024),
        )(rotated, rotations)
        return rotated, rotations, distortion.reshape(())

    rows = P(("grp", "peer"), None)
    cells = P(("grp", "peer"), None, None)
    return jax.shard_map(
        local,
        mesh=mesh,
        in_specs=(rows, P(("grp", "peer")), rows, rows, cells),
        out_specs=(rows, cells, P()),
        check_vma=False,
    )
```

```python
import jax
import jax.numpy as jnp
from jax import lax
from jax.experimental import pallas as pl
from jax.experimental.pallas import tpu as pltpu
from jax.sharding import PartitionSpec as P

MESH = pl.DeviceIdType.MESH
NEWTON = 3
D = 256
HALF = 128
SUB = 32
CODES = 256
ROWS_DEV = 256
OWN = 10
X_SIZE, Y_SIZE = 4, 8
PEERS = X_SIZE * Y_SIZE
MSG = 24
SLOT = 16
CHUNK = 8
CHUNKS = PEERS // CHUNK
CORES = 2
HUB_PLANES = 4
CROWS = CHUNK * SLOT
CMSG = CHUNK * MSG
F32, BF16, I32 = jnp.float32, jnp.bfloat16, jnp.int32


def hops(delta):
    y, x = delta // X_SIZE, delta % X_SIZE
    return min(y, Y_SIZE - y) + min(x, X_SIZE - x)


FAR_FIRST = sorted(range(1, PEERS), key=lambda delta: -hops(delta))
CHUNK_ORDER = ((2, 1, 3, 0),)


def nn(a, b):
    return jnp.dot(a, b, preferred_element_type=F32)


def nt(a, b):
    return lax.dot_general(a, b, (((1,), (1,)), ((), ())), preferred_element_type=F32)


def iota(shape, dim):
    return lax.broadcasted_iota(I32, shape, dim)


def hot(mask):
    return mask.astype(F32).astype(BF16)


def drain(ref, sem):
    pltpu.make_async_copy(ref, ref, sem.at[0]).wait()


def kernel(
    groups,
    desc_hbm,
    cell_hbm,
    code_hbm,
    cent_hbm,
    book_hbm,
    rotated_ref,
    rot_ref,
    dist_ref,
    desc_ref,
    cell_ref,
    code_ref,
    cent_ref,
    book_ref,
    load_sem,
    send,
    got,
    back,
    ret,
    table,
    rebuilt,
    resid,
    decoded,
    perm_t,
    err_mine,
    err_grp,
    err_sum,
    err_peer,
    err_total,
    out_sem,
    in_sem,
    back_sem,
    ret_sem,
    eg_out,
    eg_in,
    ep_out,
    ep_in,
    et_out,
    et_in,
):
    me_g = lax.axis_index("grp")
    me_p = lax.axis_index("peer")
    my_y, my_x = me_p // X_SIZE, me_p % X_SIZE
    core, plane = me_g % CORES, me_g // CORES
    hubs = min(HUB_PLANES * CORES, groups)
    far = range(HUB_PLANES, groups // CORES)
    is_hub = me_g < hubs
    is_relay = plane == HUB_PLANES - 1
    greeted = PEERS - 1 + jnp.where(is_hub, hubs - 1, hubs) + jnp.where(is_relay, len(far), 0)

    def ahead(delta):
        to_y = (my_y + delta // X_SIZE) % Y_SIZE
        to_x = (my_x + delta % X_SIZE) % X_SIZE
        return (me_g, to_y * X_SIZE + to_x)

    def behind(delta):
        to_y = (my_y + Y_SIZE - delta // X_SIZE) % Y_SIZE
        to_x = (my_x + X_SIZE - delta % X_SIZE) % X_SIZE
        return (me_g, to_y * X_SIZE + to_x)

    def level(step):
        return ((me_g + step) % groups, me_p)

    loads = [
        pltpu.make_async_copy(src, dst, load_sem.at[i])
        for i, (src, dst) in enumerate(
            [
                (cell_hbm, cell_ref),
                (code_hbm, code_ref),
                (desc_hbm, desc_ref),
                (cent_hbm, cent_ref),
                (book_hbm, book_ref),
            ]
        )
    ]
    for load in loads:
        load.start()

    barrier = pltpu.get_barrier_semaphore()
    for delta in FAR_FIRST:
        pl.semaphore_signal(barrier, inc=1, device_id=ahead(delta), device_id_type=MESH)

    @pl.when(is_hub)
    def _():
        for step in range(1, groups):
            pl.semaphore_signal(barrier, inc=1, device_id=level(step), device_id_type=MESH)

    @pl.when(jnp.logical_not(is_hub))
    def _():
        relay = ((HUB_PLANES - 1) * CORES + core, me_p)
        pl.semaphore_signal(barrier, inc=1, device_id=relay, device_id_type=MESH)

    loads[0].wait()
    cell = cell_ref[...]
    owner = cell >> 1
    rel = (((owner >> 2) - my_y) & (Y_SIZE - 1)) * X_SIZE + (((owner & 3) - my_x) & (X_SIZE - 1))
    owned = iota((PEERS, ROWS_DEV), 0) == rel
    earlier = hot(iota((ROWS_DEV, ROWS_DEV), 0) < iota((ROWS_DEV, ROWS_DEV), 1))
    count = nn(hot(owned), earlier)
    rank = jnp.sum(jnp.where(owned, count, 0.0), axis=0, keepdims=True).astype(I32)
    low = rel * MSG + rank
    position = iota((PEERS * MSG, ROWS_DEV), 0)
    loads[1].wait()
    code = code_ref[...] + 1
    signed = jnp.where((cell & 1) == 1, -code, code).astype(F32)
    spread = jnp.concatenate(
        [jnp.where((rank & 3) == k, signed, 0.0) for k in range(4)], axis=0
    ).astype(BF16)
    loads[2].wait()
    packed = (
        nn(hot(position == low), desc_ref[:, :HALF])
        + nn(hot(position == low + OWN), desc_ref[:, HALF:])
        + nt(hot(position == rel * MSG + 2 * OWN + (rank >> 2)), spread)
    )
    send[...] = packed.astype(BF16).reshape(PEERS, MSG, HALF)

    pl.semaphore_wait(barrier, greeted)

    def out_copy(delta):
        return pltpu.make_async_remote_copy(
            src_ref=send.at[delta],
            dst_ref=got.at[delta],
            send_sem=out_sem.at[0],
            recv_sem=in_sem.at[delta // CHUNK],
            device_id=ahead(delta),
            device_id_type=MESH,
        )

    for delta in FAR_FIRST:
        out_copy(delta).start()
    got[0] = send[0]

    place = rel * SLOT + rank
    place_col = jnp.broadcast_to(place.astype(F32), (8, ROWS_DEV)).T[:, :1].astype(I32)
    perm_t[...] = hot(iota((ROWS_DEV, PEERS * SLOT), 1) == place_col)
    loads[3].wait()
    loads[4].wait()
    for c in range(2):
        table[c] = book_ref[c].astype(F32).T
    cent = cent_ref[...].astype(F32)

    row = iota((CROWS, CMSG), 0)
    source, slot = row // SLOT, row % SLOT
    col = iota((CROWS, CMSG), 1)
    col_source, col_row = col // MSG, col % MSG
    same = (source == col_source) & (slot < OWN)
    pick_low = hot(same & (col_row == slot))
    pick_high = hot(same & (col_row == slot + OWN))
    pick_code = hot(same & (col_row == 2 * OWN + (slot >> 2)))
    own_lane = (iota((CROWS, HALF), 1) // SUB) == (iota((CROWS, HALF), 0) % SLOT) % 4
    fold = hot(iota((SUB, HALF), 1) % SUB == iota((SUB, HALF), 0))
    first = hot(iota((HALF, HALF), 0) % SUB == 0)

    def decode(chunks):
        messages = []
        for chunk in chunks:
            arrived = got.at[max(chunk * CHUNK, 1) : chunk * CHUNK + CHUNK]
            pltpu.make_async_copy(arrived, arrived, in_sem.at[chunk]).wait()
        for chunk in chunks:
            message = got[chunk * CHUNK : chunk * CHUNK + CHUNK].reshape(CMSG, HALF)
            messages.append(message)
        codes = [jnp.where(own_lane, nn(pick_code, m), 0.0).astype(BF16) for m in messages]
        code_ts = [nt(fold, x) for x in codes]
        code_cols = [nn(x, first) for x in codes]
        for chunk, message, code_t, code_col in zip(chunks, messages, code_ts, code_cols):
            here = slice(chunk * CROWS, chunk * CROWS + CROWS)
            which = (jnp.abs(code_t) - 1.0).astype(I32)
            parts = [[], []]
            for s in range(SUB):
                index = jnp.broadcast_to(which[s : s + 1], (8, CROWS))
                sign = jnp.broadcast_to(code_t[s : s + 1], (8, CROWS))
                near = index & 127
                part = slice(8 * s, 8 * s + 8)
                values = []
                for c in range(2):
                    left = table[c, part, 0:128]
                    right = table[c, part, 128:256]
                    left = jnp.take_along_axis(left, near, axis=1, mode="promise_in_bounds")
                    right = jnp.take_along_axis(right, near, axis=1, mode="promise_in_bounds")
                    value = jnp.where(index < 128, left, right)
                    valid = sign > 0.0 if c == 0 else sign < 0.0
                    values.append(jnp.where(valid, value, 0.0))
                    parts[c].append(values[c])
            rebuilt_t = [jnp.concatenate(p, axis=0) for p in parts]
            for c in range(2):
                decoded[c, :, here] = rebuilt_t[c].astype(BF16)
            rebuilt[here] = (rebuilt_t[0] + rebuilt_t[1]).T
            rows = jnp.concatenate([nn(pick_low, message), nn(pick_high, message)], axis=1)
            keep = [code_col > 0.0, code_col < 0.0]
            for c in range(2):
                both = jnp.concatenate([keep[c], keep[c]], axis=1)
                resid[here, c * D : c * D + D] = jnp.where(both, rows - cent[c : c + 1], 0.0).astype(BF16)

    for chunks in CHUNK_ORDER:
        decode(chunks)

    cov = [nn(decoded[c], resid[:, c * D : c * D + D]) for c in range(2)]
    inverse = [lax.rsqrt(jnp.sum(m * m, keepdims=True) + 1e-06) for m in cov]
    small = [m.astype(BF16) for m in cov]
    gram = [(nt(b, b) * (i * i)).astype(BF16) for b, i in zip(small, inverse)]
    polar = [i * (1.5 * m - 0.5 * nn(g, b)) for m, g, b, i in zip(cov, gram, small, inverse)]
    for _ in range(NEWTON - 1):
        small = [q.astype(BF16) for q in polar]
        gram = [nt(b, b).astype(BF16) for b in small]
        polar = [1.5 * q - 0.5 * nn(g, b) for q, g, b in zip(polar, gram, small)]
    turn = [q.astype(BF16) for q in polar]

    turned = nt(resid[...], jnp.concatenate(turn, axis=1))
    off = turned - rebuilt[...]
    total = jnp.sum(off * off, axis=0, keepdims=True)
    err_mine[...] = total[:, :HALF] + total[:, HALF:]

    def hub_copy(hub):
        return pltpu.make_async_remote_copy(
            src_ref=err_mine,
            dst_ref=err_grp.at[(me_g + groups - hub) % groups],
            send_sem=eg_out.at[0],
            recv_sem=eg_in.at[0],
            device_id=(hub, me_p),
            device_id_type=MESH,
        )

    def total_copy(to_plane):
        return pltpu.make_async_remote_copy(
            src_ref=err_total,
            dst_ref=err_total,
            send_sem=et_out.at[0],
            recv_sem=et_in.at[0],
            device_id=(to_plane * CORES + core, me_p),
            device_id_type=MESH,
        )

    def back_copy(delta):
        return pltpu.make_async_remote_copy(
            src_ref=back.at[delta],
            dst_ref=ret.at[delta],
            send_sem=back_sem.at[0],
            recv_sem=ret_sem.at[0],
            device_id=behind(delta),
            device_id_type=MESH,
        )

    def peer_copy(delta):
        return pltpu.make_async_remote_copy(
            src_ref=err_sum,
            dst_ref=err_peer.at[delta],
            send_sem=ep_out.at[0],
            recv_sem=ep_in.at[0],
            device_id=ahead(delta),
            device_id_type=MESH,
        )

    for hub in range(hubs):

        @pl.when(me_g != hub)
        def _():
            hub_copy(hub).start()

    back[...] = turned.astype(BF16).reshape(PEERS, SLOT, D)
    for delta in FAR_FIRST:
        back_copy(delta).start()
    err_grp[0] = err_mine[...]
    ret[0] = back[0]
    for c in range(2):
        rot_ref[c] = polar[c].T
    drain(send.at[1:PEERS], out_sem)

    @pl.when(is_hub)
    def _():
        drain(err_grp.at[1:groups], eg_in)
        err_sum[...] = jnp.sum(err_grp[...], axis=0)
        for delta in FAR_FIRST:
            peer_copy(delta).start()
        err_peer[0] = err_sum[...]
        drain(err_grp.at[1:hubs], eg_out)

    @pl.when(jnp.logical_not(is_hub))
    def _():
        drain(err_grp.at[0:hubs], eg_out)

    drain(ret.at[1:PEERS], ret_sem)
    rotated_ref[...] = nn(perm_t[...], ret[...].reshape(PEERS * SLOT, D)).astype(BF16)
    drain(back.at[1:PEERS], back_sem)

    scale = 1.0 / (ROWS_DEV * PEERS * groups * D)

    @pl.when(is_hub)
    def _():
        drain(err_peer.at[1:PEERS], ep_out)
        drain(err_peer.at[1:PEERS], ep_in)
        total = jnp.sum(err_peer[...], axis=0)
        dist_ref[0, 0] = jnp.sum(total) * scale
        err_total[...] = total

    if far:

        @pl.when(is_relay)
        def _():
            for to_plane in far:
                total_copy(to_plane).start()
            drain(err_grp.at[0 : len(far)], et_out)

        @pl.when(jnp.logical_not(is_hub))
        def _():
            drain(err_total, et_in)
            dist_ref[0, 0] = jnp.sum(err_total[...]) * scale


def place_results(rotated_in, rot_in, dist_in, rotated_out, rot_out, dist_out, held, sem):
    held[...] = jnp.full((1, 1), dist_in[0, 0], F32)
    copies = [
        pltpu.make_async_copy(rot_in, rot_out, sem.at[0]),
        pltpu.make_async_copy(rotated_in, rotated_out, sem.at[1]),
        pltpu.make_async_copy(held, dist_out, sem.at[2]),
    ]
    for copy in copies:
        copy.start()
    for copy in copies:
        copy.wait()


def solution(mesh):
    groups = mesh.shape["grp"]
    vmem = pl.BlockSpec(memory_space=pltpu.VMEM)
    smem = pl.BlockSpec(memory_space=pltpu.SMEM)
    hbm = pl.BlockSpec(memory_space=pltpu.HBM)

    def local(descriptors, cell_ids, sub_codes, centroids, codebooks):
        operands = (
            descriptors,
            cell_ids.reshape(1, ROWS_DEV),
            sub_codes.T,
            centroids,
            codebooks,
        )
        rotated, rotations, distortion = pl.pallas_call(
            lambda *refs: kernel(groups, *refs),
            out_shape=(
                pltpu.VMEM((ROWS_DEV, D), BF16),
                pltpu.VMEM((2, D, D), F32),
                pltpu.SMEM((1, 1), F32),
            ),
            in_specs=[hbm] * 5,
            out_specs=(vmem, vmem, smem),
            scratch_shapes=[
                pltpu.VMEM((ROWS_DEV, D), BF16),
                pltpu.VMEM((1, ROWS_DEV), I32),
                pltpu.VMEM((SUB, ROWS_DEV), I32),
                pltpu.VMEM((2, D), BF16),
                pltpu.VMEM((2, CODES, D), BF16),
                pltpu.SemaphoreType.DMA((5,)),
                pltpu.VMEM((PEERS, MSG, HALF), BF16),
                pltpu.VMEM((PEERS, MSG, HALF), BF16),
                pltpu.VMEM((PEERS, SLOT, D), BF16),
                pltpu.VMEM((PEERS, SLOT, D), BF16),
                pltpu.VMEM((2, D, CODES), F32),
                pltpu.VMEM((PEERS * SLOT, D), F32),
                pltpu.VMEM((PEERS * SLOT, 2 * D), BF16),
                pltpu.VMEM((2, D, PEERS * SLOT), BF16),
                pltpu.VMEM((ROWS_DEV, PEERS * SLOT), BF16),
                pltpu.VMEM((1, HALF), F32),
                pltpu.VMEM((groups, 1, HALF), F32),
                pltpu.VMEM((1, HALF), F32),
                pltpu.VMEM((PEERS, 1, HALF), F32),
                pltpu.VMEM((1, HALF), F32),
                pltpu.SemaphoreType.DMA((1,)),
                pltpu.SemaphoreType.DMA((CHUNKS,)),
                pltpu.SemaphoreType.DMA((1,)),
                pltpu.SemaphoreType.DMA((1,)),
                pltpu.SemaphoreType.DMA((1,)),
                pltpu.SemaphoreType.DMA((1,)),
                pltpu.SemaphoreType.DMA((1,)),
                pltpu.SemaphoreType.DMA((1,)),
                pltpu.SemaphoreType.DMA((1,)),
                pltpu.SemaphoreType.DMA((1,)),
            ],
            compiler_params=pltpu.CompilerParams(
                collective_id=0, has_side_effects=True, vmem_limit_bytes=32 * 1024 * 1024
            ),
        )(*(pltpu.with_memory_space_constraint(x, pltpu.HBM) for x in operands))
        rotated, rotations, distortion = pl.pallas_call(
            place_results,
            out_shape=(
                pltpu.HBM((ROWS_DEV, D), BF16),
                pltpu.HBM((2, D, D), F32),
                pltpu.HBM((1, 1), F32),
            ),
            in_specs=[pl.BlockSpec(memory_space=pl.ANY)] * 2 + [smem],
            out_specs=(hbm,) * 3,
            scratch_shapes=[pltpu.VMEM((1, 1), F32), pltpu.SemaphoreType.DMA((3,))],
            compiler_params=pltpu.CompilerParams(vmem_limit_bytes=1024 * 1024),
        )(rotated, rotations, distortion)
        return rotated, rotations, distortion.reshape(())

    rows = P(("grp", "peer"), None)
    cells = P(("grp", "peer"), None, None)
    return jax.shard_map(
        local,
        mesh=mesh,
        in_specs=(rows, P(("grp", "peer")), rows, rows, cells),
        out_specs=(rows, cells, P()),
        check_vma=False,
    )
```

```python
import jax
import jax.numpy as jnp
from jax import lax
from jax.experimental import pallas as pl
from jax.experimental.pallas import tpu as pltpu
from jax.sharding import PartitionSpec as P

MESH = pl.DeviceIdType.MESH
NEWTON = 3
D = 256
HALF = 128
SUB = 32
CODES = 256
ROWS_DEV = 256
OWN = 10
X_SIZE, Y_SIZE = 4, 8
PEERS = X_SIZE * Y_SIZE
MSG = 24
SLOT = 16
CHUNK = 12
CHUNKS = 3
CORES = 2
HUB_PLANES = 4
CROWS = 128
ROWS = CHUNKS * CROWS
CMSG = CHUNK * MSG
F32, BF16, I32 = jnp.float32, jnp.bfloat16, jnp.int32


def hops(delta):
    y, x = delta // X_SIZE, delta % X_SIZE
    return min(y, Y_SIZE - y) + min(x, X_SIZE - x)


FAR_FIRST = sorted(range(1, PEERS), key=lambda delta: -hops(delta))
CHUNK_ORDER = ((0, 1, 2),)


def nn(a, b):
    return jnp.dot(a, b, preferred_element_type=F32)


def nt(a, b):
    return lax.dot_general(a, b, (((1,), (1,)), ((), ())), preferred_element_type=F32)


def iota(shape, dim):
    return lax.broadcasted_iota(I32, shape, dim)


def hot(mask):
    return mask.astype(F32).astype(BF16)


def drain(ref, sem):
    pltpu.make_async_copy(ref, ref, sem.at[0]).wait()


def kernel(
    groups,
    desc_hbm,
    cell_hbm,
    code_hbm,
    cent_hbm,
    book_hbm,
    rotated_ref,
    rot_ref,
    dist_ref,
    desc_ref,
    cell_ref,
    code_ref,
    cent_ref,
    book_ref,
    load_sem,
    send,
    got,
    back,
    ret,
    table,
    rebuilt,
    resid,
    decoded,
    spread_out,
    perm_t,
    err_mine,
    err_grp,
    err_sum,
    err_peer,
    err_total,
    out_sem,
    in_sem,
    back_sem,
    ret_sem,
    eg_out,
    eg_in,
    ep_out,
    ep_in,
    et_out,
    et_in,
):
    me_g = lax.axis_index("grp")
    me_p = lax.axis_index("peer")
    my_y, my_x = me_p // X_SIZE, me_p % X_SIZE
    core, plane = me_g % CORES, me_g // CORES
    hubs = min(HUB_PLANES * CORES, groups)
    far = range(HUB_PLANES, groups // CORES)
    is_hub = me_g < hubs
    is_relay = plane == HUB_PLANES - 1
    greeted = PEERS - 1 + jnp.where(is_hub, hubs - 1, hubs) + jnp.where(is_relay, len(far), 0)

    def ahead(delta):
        to_y = (my_y + delta // X_SIZE) % Y_SIZE
        to_x = (my_x + delta % X_SIZE) % X_SIZE
        return (me_g, to_y * X_SIZE + to_x)

    def behind(delta):
        to_y = (my_y + Y_SIZE - delta // X_SIZE) % Y_SIZE
        to_x = (my_x + X_SIZE - delta % X_SIZE) % X_SIZE
        return (me_g, to_y * X_SIZE + to_x)

    def level(step):
        return ((me_g + step) % groups, me_p)

    loads = [
        pltpu.make_async_copy(src, dst, load_sem.at[i])
        for i, (src, dst) in enumerate(
            [
                (cell_hbm, cell_ref),
                (code_hbm, code_ref),
                (desc_hbm, desc_ref),
                (cent_hbm, cent_ref),
                (book_hbm, book_ref),
            ]
        )
    ]
    for load in loads:
        load.start()

    barrier = pltpu.get_barrier_semaphore()
    for delta in FAR_FIRST:
        pl.semaphore_signal(barrier, inc=1, device_id=ahead(delta), device_id_type=MESH)

    @pl.when(is_hub)
    def _():
        for step in range(1, groups):
            pl.semaphore_signal(barrier, inc=1, device_id=level(step), device_id_type=MESH)

    @pl.when(jnp.logical_not(is_hub))
    def _():
        relay = ((HUB_PLANES - 1) * CORES + core, me_p)
        pl.semaphore_signal(barrier, inc=1, device_id=relay, device_id_type=MESH)

    loads[0].wait()
    cell = cell_ref[...]
    owner = cell >> 1
    rel = (((owner >> 2) - my_y) & (Y_SIZE - 1)) * X_SIZE + (((owner & 3) - my_x) & (X_SIZE - 1))
    owned = iota((PEERS, ROWS_DEV), 0) == rel
    earlier = hot(iota((ROWS_DEV, ROWS_DEV), 0) < iota((ROWS_DEV, ROWS_DEV), 1))
    count = nn(hot(owned), earlier)
    rank = jnp.sum(jnp.where(owned, count, 0.0), axis=0, keepdims=True).astype(I32)
    low = rel * MSG + rank
    position = iota((PEERS * MSG, ROWS_DEV), 0)
    loads[1].wait()
    code = code_ref[...] + 1
    signed = jnp.where((cell & 1) == 1, -code, code).astype(F32)
    spread = jnp.concatenate(
        [jnp.where((rank & 3) == k, signed, 0.0) for k in range(4)], axis=0
    ).astype(BF16)
    loads[2].wait()
    packed = (
        nn(hot(position == low), desc_ref[:, :HALF])
        + nn(hot(position == low + OWN), desc_ref[:, HALF:])
        + nt(hot(position == rel * MSG + 2 * OWN + (rank >> 2)), spread)
    )
    send[...] = packed.astype(BF16).reshape(PEERS, MSG, HALF)

    pl.semaphore_wait(barrier, greeted)

    def out_copy(delta):
        return pltpu.make_async_remote_copy(
            src_ref=send.at[delta],
            dst_ref=got.at[delta],
            send_sem=out_sem.at[0],
            recv_sem=in_sem.at[delta // CHUNK],
            device_id=ahead(delta),
            device_id_type=MESH,
        )

    for delta in FAR_FIRST:
        out_copy(delta).start()
    got[0] = send[0]
    got[PEERS:] = jnp.zeros((CHUNKS * CHUNK - PEERS, MSG, HALF), BF16)

    place = rel * SLOT + rank
    place_col = jnp.broadcast_to(place.astype(F32), (8, ROWS_DEV)).T[:, :1].astype(I32)
    perm_t[...] = hot(iota((ROWS_DEV, PEERS * SLOT), 1) == place_col)
    loads[3].wait()
    loads[4].wait()
    for c in range(2):
        table[c] = book_ref[c].astype(F32).T
    cent = cent_ref[...].astype(F32)

    row = iota((CROWS, CMSG), 0)
    source, slot = row // OWN, row % OWN
    col = iota((CROWS, CMSG), 1)
    col_source, col_row = col // MSG, col % MSG
    same = source == col_source
    pick_low = hot(same & (col_row == slot))
    pick_high = hot(same & (col_row == slot + OWN))
    pick_code = hot(same & (col_row == 2 * OWN + (slot >> 2)))
    own_lane = (iota((CROWS, HALF), 1) // SUB) == (iota((CROWS, HALF), 0) % OWN) % 4
    target = iota((PEERS * SLOT, 1), 0)
    partner, slot = target // SLOT, target % SLOT
    packed_row = (partner // CHUNK) * CROWS + (partner % CHUNK) * OWN + slot
    spread_out[...] = hot((iota((PEERS * SLOT, ROWS), 1) == packed_row) & (slot < OWN))
    fold = hot(iota((SUB, HALF), 1) % SUB == iota((SUB, HALF), 0))
    first = hot(iota((HALF, HALF), 0) % SUB == 0)

    def decode(chunks):
        messages = []
        for chunk in chunks:
            arrived = got.at[max(chunk * CHUNK, 1) : min(chunk * CHUNK + CHUNK, PEERS)]
            pltpu.make_async_copy(arrived, arrived, in_sem.at[chunk]).wait()
        for chunk in chunks:
            message = got[chunk * CHUNK : chunk * CHUNK + CHUNK].reshape(CMSG, HALF)
            messages.append(message)
        codes = [jnp.where(own_lane, nn(pick_code, m), 0.0).astype(BF16) for m in messages]
        code_ts = [nt(fold, x) for x in codes]
        code_cols = [nn(x, first) for x in codes]
        for chunk, message, code_t, code_col in zip(chunks, messages, code_ts, code_cols):
            here = slice(chunk * CROWS, chunk * CROWS + CROWS)
            which = (jnp.abs(code_t) - 1.0).astype(I32)
            parts = [[], []]
            for s in range(SUB):
                index = jnp.broadcast_to(which[s : s + 1], (8, CROWS))
                sign = jnp.broadcast_to(code_t[s : s + 1], (8, CROWS))
                near = index & 127
                part = slice(8 * s, 8 * s + 8)
                values = []
                for c in range(2):
                    left = table[c, part, 0:128]
                    right = table[c, part, 128:256]
                    left = jnp.take_along_axis(left, near, axis=1, mode="promise_in_bounds")
                    right = jnp.take_along_axis(right, near, axis=1, mode="promise_in_bounds")
                    value = jnp.where(index < 128, left, right)
                    valid = sign > 0.0 if c == 0 else sign < 0.0
                    values.append(jnp.where(valid, value, 0.0))
                    parts[c].append(values[c])
            rebuilt_t = [jnp.concatenate(p, axis=0) for p in parts]
            for c in range(2):
                decoded[c, :, here] = rebuilt_t[c].astype(BF16)
            rebuilt[here] = (rebuilt_t[0] + rebuilt_t[1]).T
            rows = jnp.concatenate([nn(pick_low, message), nn(pick_high, message)], axis=1)
            keep = [code_col > 0.0, code_col < 0.0]
            for c in range(2):
                both = jnp.concatenate([keep[c], keep[c]], axis=1)
                resid[here, c * D : c * D + D] = jnp.where(both, rows - cent[c : c + 1], 0.0).astype(BF16)

    for chunks in CHUNK_ORDER:
        decode(chunks)

    cov = [nn(decoded[c], resid[:, c * D : c * D + D]) for c in range(2)]
    inverse = [lax.rsqrt(jnp.sum(m * m, keepdims=True) + 1e-06) for m in cov]
    small = [m.astype(BF16) for m in cov]
    gram = [(nt(b, b) * (i * i)).astype(BF16) for b, i in zip(small, inverse)]
    polar = [i * (1.5 * m - 0.5 * nn(g, b)) for m, g, b, i in zip(cov, gram, small, inverse)]
    for _ in range(NEWTON - 1):
        small = [q.astype(BF16) for q in polar]
        gram = [nt(b, b).astype(BF16) for b in small]
        polar = [1.5 * q - 0.5 * nn(g, b) for q, g, b in zip(polar, gram, small)]
    turn = [q.astype(BF16) for q in polar]

    turned = nt(resid[...], jnp.concatenate(turn, axis=1))
    off = turned - rebuilt[...]
    total = jnp.sum(off * off, axis=0, keepdims=True)
    err_mine[...] = total[:, :HALF] + total[:, HALF:]

    def hub_copy(hub):
        return pltpu.make_async_remote_copy(
            src_ref=err_mine,
            dst_ref=err_grp.at[(me_g + groups - hub) % groups],
            send_sem=eg_out.at[0],
            recv_sem=eg_in.at[0],
            device_id=(hub, me_p),
            device_id_type=MESH,
        )

    def total_copy(to_plane):
        return pltpu.make_async_remote_copy(
            src_ref=err_total,
            dst_ref=err_total,
            send_sem=et_out.at[0],
            recv_sem=et_in.at[0],
            device_id=(to_plane * CORES + core, me_p),
            device_id_type=MESH,
        )

    def back_copy(delta):
        return pltpu.make_async_remote_copy(
            src_ref=back.at[delta],
            dst_ref=ret.at[delta],
            send_sem=back_sem.at[0],
            recv_sem=ret_sem.at[0],
            device_id=behind(delta),
            device_id_type=MESH,
        )

    def peer_copy(delta):
        return pltpu.make_async_remote_copy(
            src_ref=err_sum,
            dst_ref=err_peer.at[delta],
            send_sem=ep_out.at[0],
            recv_sem=ep_in.at[0],
            device_id=ahead(delta),
            device_id_type=MESH,
        )

    for hub in range(hubs):

        @pl.when(me_g != hub)
        def _():
            hub_copy(hub).start()

    back[...] = nn(spread_out[...], turned.astype(BF16)).astype(BF16).reshape(PEERS, SLOT, D)
    for delta in FAR_FIRST:
        back_copy(delta).start()
    err_grp[0] = err_mine[...]
    ret[0] = back[0]
    for c in range(2):
        rot_ref[c] = polar[c].T
    drain(send.at[1:PEERS], out_sem)

    @pl.when(is_hub)
    def _():
        drain(err_grp.at[1:groups], eg_in)
        err_sum[...] = jnp.sum(err_grp[...], axis=0)
        for delta in FAR_FIRST:
            peer_copy(delta).start()
        err_peer[0] = err_sum[...]
        drain(err_grp.at[1:hubs], eg_out)

    @pl.when(jnp.logical_not(is_hub))
    def _():
        drain(err_grp.at[0:hubs], eg_out)

    drain(ret.at[1:PEERS], ret_sem)
    rotated_ref[...] = nn(perm_t[...], ret[...].reshape(PEERS * SLOT, D)).astype(BF16)
    drain(back.at[1:PEERS], back_sem)

    scale = 1.0 / (ROWS_DEV * PEERS * groups * D)

    @pl.when(is_hub)
    def _():
        drain(err_peer.at[1:PEERS], ep_out)
        drain(err_peer.at[1:PEERS], ep_in)
        total = jnp.sum(err_peer[...], axis=0)
        dist_ref[0, 0] = jnp.sum(total) * scale
        err_total[...] = total

    if far:

        @pl.when(is_relay)
        def _():
            for to_plane in far:
                total_copy(to_plane).start()
            drain(err_grp.at[0 : len(far)], et_out)

        @pl.when(jnp.logical_not(is_hub))
        def _():
            drain(err_total, et_in)
            dist_ref[0, 0] = jnp.sum(err_total[...]) * scale


def place_results(rotated_in, rot_in, dist_in, rotated_out, rot_out, dist_out, held, sem):
    held[...] = jnp.full((1, 1), dist_in[0, 0], F32)
    copies = [
        pltpu.make_async_copy(rot_in, rot_out, sem.at[0]),
        pltpu.make_async_copy(rotated_in, rotated_out, sem.at[1]),
        pltpu.make_async_copy(held, dist_out, sem.at[2]),
    ]
    for copy in copies:
        copy.start()
    for copy in copies:
        copy.wait()


def solution(mesh):
    groups = mesh.shape["grp"]
    vmem = pl.BlockSpec(memory_space=pltpu.VMEM)
    smem = pl.BlockSpec(memory_space=pltpu.SMEM)
    hbm = pl.BlockSpec(memory_space=pltpu.HBM)

    def local(descriptors, cell_ids, sub_codes, centroids, codebooks):
        operands = (
            descriptors,
            cell_ids.reshape(1, ROWS_DEV),
            sub_codes.T,
            centroids,
            codebooks,
        )
        rotated, rotations, distortion = pl.pallas_call(
            lambda *refs: kernel(groups, *refs),
            out_shape=(
                pltpu.VMEM((ROWS_DEV, D), BF16),
                pltpu.VMEM((2, D, D), F32),
                pltpu.SMEM((1, 1), F32),
            ),
            in_specs=[hbm] * 5,
            out_specs=(vmem, vmem, smem),
            scratch_shapes=[
                pltpu.VMEM((ROWS_DEV, D), BF16),
                pltpu.VMEM((1, ROWS_DEV), I32),
                pltpu.VMEM((SUB, ROWS_DEV), I32),
                pltpu.VMEM((2, D), BF16),
                pltpu.VMEM((2, CODES, D), BF16),
                pltpu.SemaphoreType.DMA((5,)),
                pltpu.VMEM((PEERS, MSG, HALF), BF16),
                pltpu.VMEM((CHUNKS * CHUNK, MSG, HALF), BF16),
                pltpu.VMEM((PEERS, SLOT, D), BF16),
                pltpu.VMEM((PEERS, SLOT, D), BF16),
                pltpu.VMEM((2, D, CODES), F32),
                pltpu.VMEM((ROWS, D), F32),
                pltpu.VMEM((ROWS, 2 * D), BF16),
                pltpu.VMEM((2, D, ROWS), BF16),
                pltpu.VMEM((PEERS * SLOT, ROWS), BF16),
                pltpu.VMEM((ROWS_DEV, PEERS * SLOT), BF16),
                pltpu.VMEM((1, HALF), F32),
                pltpu.VMEM((groups, 1, HALF), F32),
                pltpu.VMEM((1, HALF), F32),
                pltpu.VMEM((PEERS, 1, HALF), F32),
                pltpu.VMEM((1, HALF), F32),
                pltpu.SemaphoreType.DMA((1,)),
                pltpu.SemaphoreType.DMA((CHUNKS,)),
                pltpu.SemaphoreType.DMA((1,)),
                pltpu.SemaphoreType.DMA((1,)),
                pltpu.SemaphoreType.DMA((1,)),
                pltpu.SemaphoreType.DMA((1,)),
                pltpu.SemaphoreType.DMA((1,)),
                pltpu.SemaphoreType.DMA((1,)),
                pltpu.SemaphoreType.DMA((1,)),
                pltpu.SemaphoreType.DMA((1,)),
            ],
            compiler_params=pltpu.CompilerParams(
                collective_id=0, has_side_effects=True, vmem_limit_bytes=32 * 1024 * 1024
            ),
        )(*(pltpu.with_memory_space_constraint(x, pltpu.HBM) for x in operands))
        rotated, rotations, distortion = pl.pallas_call(
            place_results,
            out_shape=(
                pltpu.HBM((ROWS_DEV, D), BF16),
                pltpu.HBM((2, D, D), F32),
                pltpu.HBM((1, 1), F32),
            ),
            in_specs=[pl.BlockSpec(memory_space=pl.ANY)] * 2 + [smem],
            out_specs=(hbm,) * 3,
            scratch_shapes=[pltpu.VMEM((1, 1), F32), pltpu.SemaphoreType.DMA((3,))],
            compiler_params=pltpu.CompilerParams(vmem_limit_bytes=1024 * 1024),
        )(rotated, rotations, distortion)
        return rotated, rotations, distortion.reshape(())

    rows = P(("grp", "peer"), None)
    cells = P(("grp", "peer"), None, None)
    return jax.shard_map(
        local,
        mesh=mesh,
        in_specs=(rows, P(("grp", "peer")), rows, rows, cells),
        out_specs=(rows, cells, P()),
        check_vma=False,
    )
```
